512 devices in a mesh: pipe: 2 (over core), row: 16 (over z), col: 16 (over y, x).
Axes of the slice: x: 4, y: 4, z: 16, core: 2. Of those that a mesh axis runs over, the one named last changes fastest.
Arguments:
- fwd_in: bfloat16 [2, 512, 6144], P('pipe', 'col', 'row'), may hold values from -6 to 6
- saved_in: bfloat16 [2, 512, 6144], P('pipe', 'col', 'row'), may hold values from -6 to 6
- saved_gate: bfloat16 [2, 512, 14336], P('pipe', 'row', 'col'), may hold values from -6 to 6
- saved_up: bfloat16 [2, 512, 14336], P('pipe', 'row', 'col'), may hold values from -6 to 6
- grad_out: bfloat16 [2, 512, 6144], P('pipe', 'col', 'row'), may hold values from -6 to 6
- w_gate: bfloat16 [2, 6144, 14336], P('pipe', 'row', 'col'), may hold values from -0.109375 to 0.109375
- w_up: bfloat16 [2, 6144, 14336], P('pipe', 'row', 'col'), may hold values from -0.109375 to 0.109375
- w_down: bfloat16 [2, 6144, 14336], P('pipe', 'row', 'col'), may hold values from -0.0625 to 0.0625
- mask_gate: int32 [2, 48, 112], P('pipe', 'row', 'col'), may hold values 0 or 1
- mask_up: int32 [2, 48, 112], P('pipe', 'row', 'col'), may hold values 0 or 1
- mask_down: int32 [2, 48, 112], P('pipe', 'row', 'col'), may hold values 0 or 1
- counts: int32 [2], replicated, may hold values from 256 to 512, as said below
Outputs:
- handoff: bfloat16 [2, 512, 6144], P('pipe', 'col', 'row')
- outward: bfloat16 [2, 512, 6144], P('pipe', 'col', 'row')
- grad_gate: bfloat16 [2, 6144, 14336], P('pipe', 'row', 'col')
- grad_up: bfloat16 [2, 6144, 14336], P('pipe', 'row', 'col')
- grad_down: bfloat16 [2, 6144, 14336], P('pipe', 'row', 'col')
The draws below stay inside these ranges and needn't reach their ends.
Inputs may be any that keep to these rules, and one draw needn't show every extreme that they name: counts[0] and counts[1] are the numbers of valid leading tokens of the two micro-batches; in every draw one of them equals 512.
All inputs are finite; a program needn't handle non-finite values. No bound on the sum of `mask_gate` or of `mask_up` or of `mask_down` on one device may be relied on, other than what follows from the above.
Results may differ from the reference program's by a relative error of at most 0.035.
Values may be sent and summed in bfloat16 or wider, within the bound.
A program may use at most 64 MiB of HBM per device.

```python
import jax
import jax.numpy as jnp
from jax import lax

D = 6144
FF = 14336
BLOCK = 128
TOKENS = 512
N_PIPE = 2
N_ROW = 16
N_COL = 16


def draw_counts(key, part):
    key = jax.random.fold_in(key, 11)
    first_key, second_key = jax.random.split(key)
    values = jax.random.randint(first_key, (2,), TOKENS // 2, TOKENS + 1)
    chosen = jax.random.randint(second_key, (), 0, 2)
    return jnp.where(jnp.arange(2) == chosen, TOKENS, values).astype(jnp.int32)


def with_ends(drawn, rng, least, largest):
    shape = drawn.shape
    index_at = [jax.random.randint(jax.random.fold_in(rng, axis), (), 0, shape[axis]) for axis in range(len(shape))]
    drawn = drawn.at[tuple(index_at)].set(least)
    longest = shape.index(max(shape))
    index_at[longest] = (index_at[longest] + 1) % shape[longest]
    return drawn.at[tuple(index_at)].set(largest)


def shard_levels(own_key, dims, cuts, least, top_value):
    level, own = 1.0, jax.random.fold_in(own_key, 6)
    for position, blocks in cuts:
        steps = jnp.exp(jax.random.uniform(jax.random.fold_in(own, position), (blocks,), jnp.float32, least / len(cuts), top_value / len(cuts)))
        level = level * jnp.repeat(steps, dims[position] // blocks).reshape([-1 if axis == position else 1 for axis in range(len(dims))])
    return level


def bell_draw(rng, shape, scale, bound, cuts=(), kind=jnp.bfloat16):
    level = shard_levels(rng, shape, cuts, -0.22, 0.18) if cuts else 1.0
    array = jax.random.normal(rng, shape, jnp.float32) * scale * level
    return jnp.minimum(jnp.maximum(array, -bound), bound).astype(kind)


def setup_inputs(seed: int = 0) -> dict:
    splits = jax.random.split(jax.random.key(seed), 13)
    return {
        "fwd_in": bell_draw(splits[0], (N_PIPE, TOKENS, D), 1.0, 6.0, ((0, 2), (1, 16), (2, 16))),
        "saved_in": bell_draw(splits[1], (N_PIPE, TOKENS, D), 1.0, 6.0, ((0, 2), (1, 16), (2, 16))),
        "saved_gate": bell_draw(splits[2], (N_PIPE, TOKENS, FF), 1.0, 6.0, ((0, 2), (1, 16), (2, 16))),
        "saved_up": bell_draw(splits[3], (N_PIPE, TOKENS, FF), 1.0, 6.0, ((0, 2), (1, 16), (2, 16))),
        "grad_out": bell_draw(splits[4], (N_PIPE, TOKENS, D), 1.0, 6.0, ((0, 2), (1, 16), (2, 16))),
        "w_gate": bell_draw(splits[5], (N_PIPE, D, FF), (D // 2) ** -0.5, 0.109375, ((0, 2), (1, 16), (2, 16))),
        "w_up": bell_draw(splits[6], (N_PIPE, D, FF), (D // 2) ** -0.5, 0.109375, ((0, 2), (1, 16), (2, 16))),
        "w_down": bell_draw(splits[7], (N_PIPE, D, FF), (FF // 2) ** -0.5, 0.0625, ((0, 2), (1, 16), (2, 16))),
        "mask_gate": with_ends((jax.random.randint(splits[8], (N_PIPE, D // BLOCK, FF // BLOCK), 0, 2) < 1).astype(jnp.int32), jax.random.fold_in(splits[8], 1), 0, 1),
        "mask_up": with_ends((jax.random.randint(splits[9], (N_PIPE, D // BLOCK, FF // BLOCK), 0, 2) < 1).astype(jnp.int32), jax.random.fold_in(splits[9], 1), 0, 1),
        "mask_down": with_ends((jax.random.randint(splits[10], (N_PIPE, D // BLOCK, FF // BLOCK), 0, 2) < 1).astype(jnp.int32), jax.random.fold_in(splits[10], 1), 0, 1),
        "counts": draw_counts(jax.random.fold_in(splits[12], 71), 0),
    }


def widen(block_mask, dtype):
    grid_rows, grid_cols = block_mask.shape
    grid = block_mask.astype(dtype)[:, None, :, None]
    return jnp.broadcast_to(grid, (grid_rows, BLOCK, grid_cols, BLOCK)).reshape(grid_rows * BLOCK, grid_cols * BLOCK)


def rounded(value):
    return lax.optimization_barrier(value.astype(jnp.bfloat16)).astype(jnp.float32)


def depth_sum(left, right, parts):
    width = left.shape[1] // parts
    total = jnp.zeros((left.shape[0], right.shape[1]), jnp.float32)
    for index in range(parts):
        piece = jnp.dot(left[:, index * width:(index + 1) * width], right[index * width:(index + 1) * width, :], preferred_element_type=jnp.float32)
        total = total + rounded(piece)
    return total


def hidden_sum(pairs, parts):
    width = pairs[0][0].shape[1] // parts
    total = jnp.zeros((pairs[0][0].shape[0], pairs[0][1].shape[0]), jnp.float32)
    for index in range(parts):
        piece = jnp.zeros_like(total)
        for left, weight in pairs:
            piece = piece + jnp.dot(left[:, index * width:(index + 1) * width], weight[:, index * width:(index + 1) * width].T, preferred_element_type=jnp.float32)
        total = total + rounded(piece)
    return total


def reference(fwd_in, saved_in, saved_gate, saved_up, grad_out, w_gate, w_up, w_down, mask_gate, mask_up, mask_down, counts):
    positions = jnp.arange(TOKENS, dtype=jnp.int32)[:, None]
    outputs_y, outputs_dx, grads_gate, grads_up, grads_down = [], [], [], [], []
    for section in range(N_PIPE):
        gate_eff = w_gate[section] * widen(mask_gate[section], jnp.bfloat16)
        up_eff = w_up[section] * widen(mask_up[section], jnp.bfloat16)
        down_eff = w_down[section] * widen(mask_down[section], jnp.bfloat16)
        inputs = fwd_in[section]
        gate_f = depth_sum(inputs, gate_eff, N_ROW)
        up_f = depth_sum(inputs, up_eff, N_ROW)
        hidden_f = (gate_f * jax.nn.sigmoid(gate_f) * up_f).astype(jnp.bfloat16)
        ffn_f = hidden_sum([(hidden_f, down_eff)], N_COL)
        output = jnp.where(positions < counts[0], inputs.astype(jnp.float32) + ffn_f, 0.0).astype(jnp.bfloat16)
        cotangent = jnp.where(positions < counts[1], grad_out[section], jnp.zeros_like(grad_out[section]))
        dhid = depth_sum(cotangent, down_eff, N_ROW)
        gate_b = saved_gate[section].astype(jnp.float32)
        up_b = saved_up[section].astype(jnp.float32)
        sigma = jax.nn.sigmoid(gate_b)
        dgate = (dhid * up_b * sigma * (1.0 + gate_b * (1.0 - sigma))).astype(jnp.bfloat16)
        grad_upv = (dhid * gate_b * sigma).astype(jnp.bfloat16)
        hidden_b = (gate_b * sigma * up_b).astype(jnp.bfloat16)
        back_sum = hidden_sum([(dgate, gate_eff), (grad_upv, up_eff)], N_COL)
        input_grad = (cotangent.astype(jnp.float32) + back_sum).astype(jnp.bfloat16)
        stored = saved_in[section]
        grads_gate.append((widen(mask_gate[section], jnp.float32) * jnp.dot(stored.T, dgate, preferred_element_type=jnp.float32)).astype(jnp.bfloat16))
        grads_up.append((widen(mask_up[section], jnp.float32) * jnp.dot(stored.T, grad_upv, preferred_element_type=jnp.float32)).astype(jnp.bfloat16))
        grads_down.append((widen(mask_down[section], jnp.float32) * jnp.dot(cotangent.T, hidden_b, preferred_element_type=jnp.float32)).astype(jnp.bfloat16))
        outputs_y.append(output)
        outputs_dx.append(input_grad)
    handoff = jnp.stack([outputs_dx[1], outputs_y[0]])
    outward = jnp.stack([outputs_dx[0], outputs_y[1]])
    return handoff, outward, jnp.stack(grads_gate), jnp.stack(grads_up), jnp.stack(grads_down)
```

```python
import functools

import jax
import jax.numpy as jnp
from jax import lax
from jax.experimental import pallas as pl
from jax.experimental.pallas import tpu as pltpu
from jax.sharding import PartitionSpec as P

BLOCK = 128
BF16 = jnp.bfloat16
F32 = jnp.float32
MESH = pl.DeviceIdType.MESH
GATE, UP, DHID, HF, DG, DU, HB = range(7)


def kernel(
    dims,
    fwd_in, saved_in, saved_gate, saved_up, grad_out,
    w_gate, w_up, w_down,
    mask_gate, mask_up, mask_down, counts,
    handoff, outward, grad_gate, grad_up, grad_down,
    fx, ct, sv, go_v, sg_v, su_v, wg_v, wu_v, wd_v,
    part, land_a, land_b, full,
    out_y, out_dx, fold_y, fold_dx, mid_y, mid_dx, tail_y, tail_dx,
    message, leaving, received, stage,
    load_sem, z_send, z_recv, g1_send, g1_recv, g2_send, g2_recv,
    p_send, p_recv, store_sem,
):
    ring, ny, nx, chunk, depth, width = dims
    half = ring // 2
    row = lax.axis_index("row")
    col = lax.axis_index("col")
    pipe = lax.axis_index("pipe")
    y, x = col // nx, lax.rem(col, nx)

    loads = [
        pltpu.make_async_copy(grad_out.at[0], go_v, load_sem.at[0]),
        pltpu.make_async_copy(saved_gate.at[0], sg_v, load_sem.at[1]),
        pltpu.make_async_copy(saved_up.at[0], su_v, load_sem.at[2]),
        pltpu.make_async_copy(fwd_in.at[0], fx.at[y, x], load_sem.at[3]),
        pltpu.make_async_copy(saved_in.at[0], sv.at[y, x], load_sem.at[4]),
        pltpu.make_async_copy(w_gate.at[0], wg_v, load_sem.at[5]),
        pltpu.make_async_copy(w_up.at[0], wu_v, load_sem.at[6]),
        pltpu.make_async_copy(w_down.at[0], wd_v, load_sem.at[7]),
    ]
    for load in loads:
        load.start()

    right, left = lax.rem(row + 1, ring), lax.rem(row + ring - 1, ring)
    barrier = pltpu.get_barrier_semaphore()
    peers = [{"row": right}, {"row": left}, {"pipe": 1 - pipe}]
    peers += [{"col": y * nx + lax.rem(x + d, nx)} for d in range(1, nx)]
    peers += [{"col": lax.rem(y + d, ny) * nx + x} for d in range(1, ny)]
    for peer in peers:
        pl.semaphore_signal(barrier, inc=1, device_id=peer, device_id_type=MESH)

    loads[0].wait()
    positions = col * chunk + lax.broadcasted_iota(jnp.int32, (chunk, depth), 0)
    ct[x, y] = jnp.where(positions < counts[1], go_v[...].astype(F32), 0.0).astype(BF16)
    loads[1].wait()
    loads[2].wait()
    gate_b, up_b = sg_v[...].astype(F32), su_v[...].astype(F32)
    full[HB - HF, 0] = (gate_b * jax.nn.sigmoid(gate_b) * up_b).astype(BF16)
    loads[3].wait()
    loads[4].wait()

    pl.semaphore_wait(barrier, len(peers))

    sends = []

    def remote(src, dst, send_sem, recv_sem, device):
        return pltpu.make_async_remote_copy(
            src_ref=src, dst_ref=dst, send_sem=send_sem, recv_sem=recv_sem,
            device_id=device, device_id_type=MESH,
        )

    def launch(copy):
        copy.start()
        sends.append(copy)

    def arms(unit):
        longer = 1 if unit % 2 == 0 else -1
        return ((longer, half), (-longer, half - 1))

    def z_copy(unit, arm, step):
        d, n = arms(unit)[arm]
        if unit <= DHID:
            src = part.at[unit, (d * (n - step)) % ring]
            dst = (land_a if arm == 0 else land_b).at[unit, step]
        else:
            src = full.at[unit - HF, (-d * step) % ring]
            dst = full.at[unit - HF, (-d * (step + 1)) % ring]
        return remote(
            src, dst, z_send.at[unit, arm, step], z_recv.at[unit, arm, step],
            {"row": right if d == 1 else left},
        )

    def z_step(unit, step):
        for arm in range(2):
            d, n = arms(unit)[arm]
            if step > 0 and step <= n:
                z_copy(unit, arm, step - 1).wait_recv()
                if unit <= DHID and step < n:
                    slot = (d * (n - step)) % ring
                    land = (land_a if arm == 0 else land_b)[unit, step - 1]
                    part[unit, slot] = (part[unit, slot].astype(F32) + land.astype(F32)).astype(BF16)
            if step < n:
                launch(z_copy(unit, arm, step))

    def reduced(unit):
        return (
            part[unit, 0].astype(F32)
            + land_a[unit, half - 1].astype(F32)
            + land_b[unit, half - 2].astype(F32)
        )

    def where_xy(a, b):
        return {"col": a * nx + b}

    def where_yx(a, b):
        return {"col": b * nx + a}

    def gather_copy(which, phase, d):
        buf, a, b, na, nb, where = (
            (fx, y, x, ny, nx, where_xy), (ct, x, y, nx, ny, where_yx), (sv, y, x, ny, nx, where_xy)
        )[which]
        if phase == 1:
            ref, device = buf.at[a, b], where(a, lax.rem(b + d, nb))
            return remote(ref, ref, g1_send.at[which, d - 1], g1_recv.at[which, d - 1], device)
        ref, device = buf.at[a], where(lax.rem(a + d, na), b)
        return remote(ref, ref, g2_send.at[which, d - 1], g2_recv.at[which, d - 1], device)

    def gather_start(which, phase):
        for d in range(1, nx):
            launch(gather_copy(which, phase, d))

    def gather_wait(which, phase):
        for d in range(1, nx):
            gather_copy(which, phase, d).wait_recv()

    def fold_copy(which, phase, d):
        buf, land, mid, tail, a, b, na, nb, where = (
            (out_y, fold_y, mid_y, tail_y, y, x, ny, nx, where_xy),
            (out_dx, fold_dx, mid_dx, tail_dx, x, y, nx, ny, where_yx),
        )[which]
        if phase == 1:
            other = lax.rem(a + d, na)
            return remote(
                buf.at[other], land.at[d - 1],
                g1_send.at[3 + which, d - 1], g1_recv.at[3 + which, d - 1], where(other, b),
            )
        other = lax.rem(b + d, nb)
        return remote(
            mid.at[other], tail.at[d - 1],
            g2_send.at[3 + which, d - 1], g2_recv.at[3 + which, d - 1], where(a, other),
        )

    def fold_start(which):
        for d in range(1, nx):
            launch(fold_copy(which, 1, d))

    def fold_middle(which):
        buf, land, mid, a = ((out_y, fold_y, mid_y, y), (out_dx, fold_dx, mid_dx, x))[which]
        for d in range(1, nx):
            fold_copy(which, 1, d).wait_recv()
        for k in range(nx):
            total = buf[a, k].astype(F32)
            for d in range(1, nx):
                total += land[d - 1, k].astype(F32)
            mid[k] = total.astype(BF16)
        for d in range(1, nx):
            launch(fold_copy(which, 2, d))

    def fold_end(which):
        mid, tail, b = ((mid_y, tail_y, x), (mid_dx, tail_dx, y))[which]
        total = mid[b].astype(F32)
        for d in range(1, nx):
            fold_copy(which, 2, d).wait_recv()
            total += tail[d - 1].astype(F32)
        return total

    def apply_mask(weight, mask):
        for i in range(depth // BLOCK):
            for k in range(width // BLOCK):
                at = (pl.ds(i * BLOCK, BLOCK), pl.ds(k * BLOCK, BLOCK))
                weight[at] = (weight[at].astype(F32) * mask[0, i, k].astype(F32)).astype(BF16)

    def place(which, j):
        t = lax.rem(row + j, ring)
        return (t // nx, lax.rem(t, nx)) if which != 1 else (lax.rem(t, nx), t // nx)

    group = min(4, ring)

    def rows_of(which, buf, start, count):
        return jnp.concatenate([buf[place(which, start + k)] for k in range(count)], axis=0)

    def partials(which, buf, targets):
        for start in range(0, ring, group):
            lhs = rows_of(which, buf, start, group)
            for unit, weight in targets:
                product = jnp.dot(lhs, weight[...], preferred_element_type=F32).astype(BF16)
                part[unit, pl.ds(start, group)] = product.reshape(group, chunk, width)

    def back_product(which, buf, pairs):
        for start in range(0, ring, group):
            total = None
            for unit, weight in pairs:
                lhs = full[unit - HF, pl.ds(start, group)].reshape(group * chunk, width)
                term = lax.dot_general(
                    lhs, weight[...], (((1,), (1,)), ((), ())), preferred_element_type=F32
                )
                total = term if total is None else total + term
            total = total.astype(BF16)
            for k in range(group):
                buf[place(which, start + k)] = total[k * chunk:(k + 1) * chunk]

    def weight_grad(which, buf, unit, mask, index, out):
        lhs = rows_of(which, buf, 0, ring)
        for k in range(0, width, BLOCK):
            rhs = full[unit - HF, :, :, pl.ds(k, BLOCK)].reshape(ring * chunk, BLOCK)
            product = lax.dot_general(
                lhs, rhs, (((0,), (0,)), ((), ())), preferred_element_type=F32
            )
            for i in range(depth // BLOCK):
                rows = pl.ds(i * BLOCK, BLOCK)
                stage[index, rows, pl.ds(k, BLOCK)] = (
                    product[i * BLOCK:(i + 1) * BLOCK] * mask[0, i, k // BLOCK].astype(F32)
                ).astype(BF16)
        store = pltpu.make_async_copy(stage.at[index], out.at[0], store_sem.at[index])
        store.start()
        return store

    stores = []

    z_step(HB, 0)
    gather_start(0, 1)
    gather_start(1, 1)
    loads[5].wait()
    apply_mask(wg_v, mask_gate)
    loads[6].wait()
    apply_mask(wu_v, mask_up)
    z_step(HB, 1)
    gather_wait(0, 1)
    gather_start(0, 2)
    gather_wait(1, 1)
    gather_start(1, 2)
    loads[7].wait()
    apply_mask(wd_v, mask_down)
    z_step(HB, 2)
    gather_wait(0, 2)
    partials(0, fx, [(GATE, wg_v), (UP, wu_v)])
    z_step(GATE, 0)
    z_step(UP, 0)
    gather_wait(1, 2)
    gather_start(2, 1)
    partials(1, ct, [(DHID, wd_v)])
    z_step(DHID, 0)
    for s in range(1, half + 1):
        z_step(GATE, s)
        z_step(UP, s)
        z_step(DHID, s)
        if s == 2:
            gather_wait(2, 1)
            gather_start(2, 2)
    gate_f, up_f = reduced(GATE), reduced(UP)
    full[0, 0] = (gate_f * jax.nn.sigmoid(gate_f) * up_f).astype(BF16)
    z_step(HF, 0)
    dhid = reduced(DHID)
    gate_b, up_b = sg_v[...].astype(F32), su_v[...].astype(F32)
    sig = jax.nn.sigmoid(gate_b)
    full[DG - HF, 0] = (dhid * up_b * sig * (1.0 + gate_b * (1.0 - sig))).astype(BF16)
    full[DU - HF, 0] = (dhid * gate_b * sig).astype(BF16)
    z_step(DG, 0)
    z_step(DU, 0)
    for s in range(1, half + 1):
        z_step(HF, s)
        z_step(DG, s)
        z_step(DU, s)
    back_product(0, out_y, [(HF, wd_v)])
    fold_start(0)
    back_product(1, out_dx, [(DG, wg_v), (DU, wu_v)])
    fold_start(1)
    z_step(HB, 3)
    gather_wait(2, 2)
    stores.append(weight_grad(2, sv, DG, mask_gate, 0, grad_gate))
    z_step(HB, 4)
    fold_middle(0)
    fold_middle(1)
    stores.append(weight_grad(2, sv, DU, mask_up, 1, grad_up))
    z_step(HB, 5)
    ffn = fold_end(0)
    result_y = jnp.where(positions < counts[0], fx[y, x].astype(F32) + ffn, 0.0).astype(BF16)
    result_dx = (ct[x, y].astype(F32) + fold_end(1)).astype(BF16)
    first = jnp.full((chunk, depth), pipe, jnp.int32) == 0
    message[...] = jnp.where(first, result_y.astype(F32), result_dx.astype(F32)).astype(BF16)
    leaving[...] = jnp.where(first, result_dx.astype(F32), result_y.astype(F32)).astype(BF16)
    swap = remote(message, received, p_send, p_recv, {"pipe": 1 - pipe})
    launch(swap)
    stores.append(pltpu.make_async_copy(leaving, outward.at[0], store_sem.at[3]))
    stores[-1].start()
    for s in range(6, half + 1):
        z_step(HB, s)
    swap.wait_recv()
    stores.append(pltpu.make_async_copy(received, handoff.at[0], store_sem.at[4]))
    stores[-1].start()
    stores.append(weight_grad(1, ct, HB, mask_down, 2, grad_down))
    for copy in sends:
        copy.wait_send()
    for store in stores:
        store.wait()


def on_device(nx, *args):
    fwd_in, saved_gate = args[0], args[2]
    _, chunk, depth = fwd_in.shape
    _, chunk_r, width = saved_gate.shape
    cols = lax.axis_size("col")
    ring = lax.axis_size("row")
    ny = cols // nx
    assert chunk == chunk_r and ring == cols and ny == nx
    half = ring // 2
    dims = (ring, ny, nx, chunk, depth, width)
    wide = (chunk, width)
    slim = (chunk, depth)
    any_spec = pl.BlockSpec(memory_space=pl.ANY)
    smem_spec = pl.BlockSpec(memory_space=pltpu.SMEM)
    weight = jax.ShapeDtypeStruct((1, depth, width), BF16)
    act = jax.ShapeDtypeStruct((1, chunk, depth), BF16)
    dma = pltpu.SemaphoreType.DMA
    return pl.pallas_call(
        functools.partial(kernel, dims),
        out_shape=(act, act, weight, weight, weight),
        in_specs=[any_spec] * 8 + [smem_spec] * 4,
        out_specs=(any_spec,) * 5,
        scratch_shapes=[
            pltpu.VMEM((ny, nx) + slim, BF16),
            pltpu.VMEM((nx, ny) + slim, BF16),
            pltpu.VMEM((ny, nx) + slim, BF16),
            pltpu.VMEM(slim, BF16),
            pltpu.VMEM(wide, BF16),
            pltpu.VMEM(wide, BF16),
            pltpu.VMEM((depth, width), BF16),
            pltpu.VMEM((depth, width), BF16),
            pltpu.VMEM((depth, width), BF16),
            pltpu.VMEM((3, ring) + wide, BF16),
            pltpu.VMEM((3, half) + wide, BF16),
            pltpu.VMEM((3, max(half - 1, 1)) + wide, BF16),
            pltpu.VMEM((4, ring) + wide, BF16),
            pltpu.VMEM((ny, nx) + slim, BF16),
            pltpu.VMEM((nx, ny) + slim, BF16),
            pltpu.VMEM((ny - 1, nx) + slim, BF16),
            pltpu.VMEM((nx - 1, ny) + slim, BF16),
            pltpu.VMEM((nx,) + slim, BF16),
            pltpu.VMEM((ny,) + slim, BF16),
            pltpu.VMEM((nx - 1,) + slim, BF16),
            pltpu.VMEM((ny - 1,) + slim, BF16),
            pltpu.VMEM(slim, BF16),
            pltpu.VMEM(slim, BF16),
            pltpu.VMEM(slim, BF16),
            pltpu.VMEM((3, depth, width), BF16),
            dma((8,)),
            dma((7, 2, half)),
            dma((7, 2, half)),
            dma((5, nx - 1)),
            dma((5, nx - 1)),
            dma((5, nx - 1)),
            dma((5, nx - 1)),
            dma,
            dma,
            dma((5,)),
        ],
        compiler_params=pltpu.CompilerParams(
            collective_id=0, has_side_effects=True, vmem_limit_bytes=48 * 1024 * 1024
        ),
    )(*args)


def solution(mesh):
    nx = 1
    while nx * nx < mesh.shape["col"]:
        nx += 1
    tokens = P("pipe", "col", "row")
    grid = P("pipe", "row", "col")
    in_specs = (tokens, tokens, grid, grid, tokens) + (grid,) * 6 + (P(),)
    out_specs = (tokens, tokens, grid, grid, grid)
    return jax.shard_map(
        functools.partial(on_device, nx), mesh=mesh, in_specs=in_specs, out_specs=out_specs, check_vma=False
    )
```

```python
import functools

import jax
import jax.numpy as jnp
from jax import lax
from jax.experimental import pallas as pl
from jax.experimental.pallas import tpu as pltpu
from jax.sharding import PartitionSpec as P

BLOCK = 128
BF16 = jnp.bfloat16
F32 = jnp.float32
MESH = pl.DeviceIdType.MESH
GATE, UP, DHID, HF, DG, DU, HB = range(7)
IN_X, IN_COT, IN_SAVED = range(3)
OUT_Y, OUT_DX = range(2)


def kernel(
    dims,
    fwd_in, saved_in, saved_gate, saved_up, grad_out,
    w_gate, w_up, w_down,
    mask_gate, mask_up, mask_down, counts,
    handoff, outward, grad_gate, grad_up, grad_down,
    acts, go_v, sg_v, su_v, weights, mask_v, mask_rows,
    part, land_a, land_b, full, turned,
    outs, out_land, message, leaving, stage,
    load_sem, z_send, z_recv, g_send, g_recv, f_send, f_recv,
    p_send, p_recv, store_sem,
):
    ring, chunk, depth, width = dims
    half = ring // 2
    row = lax.axis_index("row")
    col = lax.axis_index("col")
    pipe = lax.axis_index("pipe")

    masks = (mask_gate, mask_up, mask_down)
    moves = [
        (fwd_in.at[0], acts.at[IN_X, col]),
        (grad_out.at[0], go_v),
        (saved_gate.at[0], sg_v),
        (saved_up.at[0], su_v),
        (saved_in.at[0], acts.at[IN_SAVED, col]),
    ]
    moves += [(mask, mask_v.at[k]) for k, mask in enumerate(masks)]
    moves += [(w.at[0], weights.at[k]) for k, w in enumerate((w_gate, w_up, w_down))]
    loads = [pltpu.make_async_copy(src, dst, load_sem.at[k]) for k, (src, dst) in enumerate(moves)]
    for load in loads:
        load.start()

    right, left = lax.rem(row + 1, ring), lax.rem(row + ring - 1, ring)
    barrier = pltpu.get_barrier_semaphore()
    peers = [{"row": right}, {"row": left}, {"pipe": 1 - pipe}]
    peers += [{"col": lax.rem(col + d, ring)} for d in range(1, ring)]
    for peer in peers:
        pl.semaphore_signal(barrier, inc=1, device_id=peer, device_id_type=MESH)

    loads[1].wait()
    positions = col * chunk + lax.broadcasted_iota(jnp.int32, (chunk, depth), 0)
    acts[IN_COT, col] = jnp.where(positions < counts[1], go_v[...].astype(F32), 0.0).astype(BF16)
    loads[2].wait()
    loads[3].wait()
    gate_b, up_b = sg_v[...].astype(F32), su_v[...].astype(F32)
    full[HB - HF, 0] = (gate_b * jax.nn.sigmoid(gate_b) * up_b).astype(BF16)
    loads[0].wait()
    loads[4].wait()

    pl.semaphore_wait(barrier, len(peers))

    sends = []

    def remote(src, dst, send_sem, recv_sem, device):
        return pltpu.make_async_remote_copy(
            src_ref=src, dst_ref=dst, send_sem=send_sem, recv_sem=recv_sem,
            device_id=device, device_id_type=MESH,
        )

    def launch(copy):
        copy.start()
        sends.append(copy)

    def arms(unit):
        longer = 1 if unit % 2 == 0 else -1
        return ((longer, half), (-longer, half - 1))

    def z_copy(unit, arm, step):
        d, n = arms(unit)[arm]
        if unit <= DHID:
            src = part.at[unit, (d * (n - step)) % ring]
            dst = (land_a if arm == 0 else land_b).at[unit, step]
        else:
            src = full.at[unit - HF, (-d * step) % ring]
            dst = full.at[unit - HF, (-d * (step + 1)) % ring]
        return remote(
            src, dst, z_send.at[unit, arm, step], z_recv.at[unit, arm, step],
            {"row": right if d == 1 else left},
        )

    def z_step(unit, step):
        for arm in range(2):
            d, n = arms(unit)[arm]
            if step > 0 and step <= n:
                z_copy(unit, arm, step - 1).wait_recv()
                if unit <= DHID and step < n:
                    slot = (d * (n - step)) % ring
                    land = (land_a if arm == 0 else land_b)[unit, step - 1]
                    part[unit, slot] = (part[unit, slot].astype(F32) + land.astype(F32)).astype(BF16)
            if 0 <= step < n:
                launch(z_copy(unit, arm, step))

    def reduced(unit):
        return (
            part[unit, 0].astype(F32)
            + land_a[unit, half - 1].astype(F32)
            + land_b[unit, half - 2].astype(F32)
        )

    def gather_copy(which, d, source, target):
        ref = acts.at[which, source]
        return remote(ref, ref, g_send.at[which, d - 1], g_recv.at[which, d - 1], {"col": target})

    def gather_start(which):
        for d in range(1, ring):
            launch(gather_copy(which, d, col, lax.rem(col + d, ring)))

    def gather_wait(which):
        for d in range(1, ring):
            gather_copy(which, d, lax.rem(col + ring - d, ring), col).wait_recv()

    def fold_copy(which, j):
        owner = lax.rem(row + j, ring)
        d = lax.rem(col - owner + ring, ring)
        index = lax.max(d - 1, 0)
        return owner, remote(
            outs.at[which, j], out_land.at[which, index],
            f_send.at[which, j], f_recv.at[which, index], {"col": owner},
        )

    def fold_start(which, j):
        owner, copy = fold_copy(which, j)

        @pl.when(owner != col)
        def _():
            copy.start()

    def fold_finish(which):
        for j in range(ring):
            owner, copy = fold_copy(which, j)

            @pl.when(owner != col)
            def _():
                copy.wait_send()

    def fold_end(which):
        total = outs[which, lax.rem(col - row + ring, ring)].astype(F32)
        for d in range(1, ring):
            remote(
                outs.at[which, 0], out_land.at[which, d - 1],
                f_send.at[which, 0], f_recv.at[which, d - 1], {"col": lax.rem(col + d, ring)},
            ).wait_recv()
            total += out_land[which, d - 1].astype(F32)
        return total

    def expand_mask(k):
        for i in range(depth // BLOCK):
            row_mask = [
                jnp.broadcast_to(mask_v[k, i, :, b:b + 1].astype(F32), (1, BLOCK))
                for b in range(width // BLOCK)
            ]
            mask_rows[k, i:i + 1, :] = jnp.concatenate(row_mask, axis=1)

    def mask_row(k, i):
        return mask_rows[k, i:i + 1, :]

    def apply_mask(k):
        for i in range(depth // BLOCK):
            at = pl.ds(i * BLOCK, BLOCK)
            weights[k, at] = (weights[k, at].astype(F32) * mask_row(k, i)).astype(BF16)

    def rows_of(which, slots):
        return jnp.concatenate([acts[which, lax.rem(row + j, ring)] for j in slots], axis=0)

    quarter = ring // 4
    first_slots = [(half - quarter // 2 + k) % ring for k in range(quarter)]
    groups = [[(j + g * quarter) % ring for j in first_slots] for g in (0, 3, 1, 2)]

    def partials(which, slots, units):
        lhs = rows_of(which, slots)
        for unit in units:
            product = jnp.dot(lhs, weights[unit], preferred_element_type=F32).astype(BF16)
            for k, j in enumerate(slots):
                part[unit, j] = product[k * chunk:(k + 1) * chunk]

    def back_product(which, slots):
        total = None
        for unit, k in (((HF, 2),), ((DG, 0), (DU, 1)))[which]:
            lhs = jnp.concatenate([full[unit - HF, j] for j in slots], axis=0)
            term = lax.dot_general(
                lhs, weights[k], (((1,), (1,)), ((), ())), preferred_element_type=F32
            )
            total = term if total is None else total + term
        total = total.astype(BF16)
        for k, j in enumerate(slots):
            outs[which, j] = total[k * chunk:(k + 1) * chunk]
            fold_start(which, j)

    def turn(k, which, slots):
        turned[k, :, pl.ds(slots[0] * chunk, len(slots) * chunk)] = rows_of(which, slots).T

    def weight_grad(k, unit, index, out):
        rhs = full[unit - HF].reshape(ring * chunk, width)
        for i in range(depth // BLOCK):
            at = pl.ds(i * BLOCK, BLOCK)
            product = jnp.dot(turned[k, at], rhs, preferred_element_type=F32)
            stage[index, at] = (product * mask_row(index, i)).astype(BF16)
        store = pltpu.make_async_copy(stage.at[index], out.at[0], store_sem.at[index])
        store.start()
        stores.append(store)

    stores = []

    gather_start(IN_X)
    z_step(HB, 0)
    gather_start(IN_COT)
    for k in range(3):
        loads[5 + k].wait()
        expand_mask(k)
    for k in range(2):
        loads[8 + k].wait()
        apply_mask(k)
    z_step(HB, 1)
    loads[10].wait()
    apply_mask(2)
    gather_wait(IN_X)
    partials(IN_X, groups[0], (GATE, UP))
    z_step(GATE, 0)
    z_step(UP, 0)
    for slots in groups[1:]:
        partials(IN_X, slots, (GATE, UP))
    z_step(HB, 2)
    gather_wait(IN_COT)
    partials(IN_COT, groups[0], (DHID,))
    z_step(DHID, 0)
    for slots in groups[1:]:
        partials(IN_COT, slots, (DHID,))
    gather_start(IN_SAVED)
    for s in range(1, half + 1):
        z_step(GATE, s)
        z_step(UP, s)
        if s < half:
            z_step(DHID, s)
        if s == 1:
            z_step(HB, 3)
        if s == 2:
            for g in range(0, ring, quarter):
                turn(0, IN_COT, range(g, g + quarter))
        if s == min(3, half):
            gather_wait(IN_SAVED)
            for g in range(0, ring, quarter):
                turn(1, IN_SAVED, range(g, g + quarter))
    gate_f, up_f = reduced(GATE), reduced(UP)
    full[0, 0] = (gate_f * jax.nn.sigmoid(gate_f) * up_f).astype(BF16)
    z_step(HF, 0)
    z_step(DHID, half)
    dhid = reduced(DHID)
    gate_b, up_b = sg_v[...].astype(F32), su_v[...].astype(F32)
    sig = jax.nn.sigmoid(gate_b)
    full[DG - HF, 0] = (dhid * up_b * sig * (1.0 + gate_b * (1.0 - sig))).astype(BF16)
    full[DU - HF, 0] = (dhid * gate_b * sig).astype(BF16)
    z_step(DG, 0)
    z_step(DU, 0)
    z_step(HB, 4)
    pending = [0]
    for s in range(1, half + 1):
        z_step(HF, s)
        z_step(DG, s)
        z_step(DU, s)
        pending += [s, ring - s] if s < half else [s]
        if s % 2 == 0 or s >= half - 1:
            back_product(OUT_Y, pending)
            back_product(OUT_DX, pending)
            pending = []
    z_step(HB, 5)
    weight_grad(1, DG, 0, grad_gate)
    z_step(HB, 6)
    ffn = fold_end(OUT_Y)
    back = fold_end(OUT_DX)
    result_y = jnp.where(positions < counts[0], acts[IN_X, col].astype(F32) + ffn, 0.0).astype(BF16)
    result_dx = (acts[IN_COT, col].astype(F32) + back).astype(BF16)
    first = jnp.full((chunk, depth), pipe, jnp.int32) == 0
    message[...] = jnp.where(first, result_y.astype(F32), result_dx.astype(F32)).astype(BF16)
    leaving[...] = jnp.where(first, result_dx.astype(F32), result_y.astype(F32)).astype(BF16)
    swap = remote(message, handoff.at[0], p_send, p_recv, {"pipe": 1 - pipe})
    launch(swap)
    stores.append(pltpu.make_async_copy(leaving, outward.at[0], store_sem.at[3]))
    stores[-1].start()
    z_step(HB, 7)
    weight_grad(1, DU, 1, grad_up)
    z_step(HB, 8)
    weight_grad(0, HB, 2, grad_down)
    swap.wait_recv()
    for copy in sends:
        copy.wait_send()
    fold_finish(OUT_Y)
    fold_finish(OUT_DX)
    for store in stores:
        store.wait()


def on_device(*args):
    fwd_in, saved_gate = args[0], args[2]
    _, chunk, depth = fwd_in.shape
    _, chunk_r, width = saved_gate.shape
    ring = lax.axis_size("row")
    assert chunk == chunk_r and ring == lax.axis_size("col")
    half = ring // 2
    dims = (ring, chunk, depth, width)
    wide = (chunk, width)
    slim = (chunk, depth)
    blocks = (depth // BLOCK, width // BLOCK)
    hbm_spec = pl.BlockSpec(memory_space=pltpu.HBM)
    smem_spec = pl.BlockSpec(memory_space=pltpu.SMEM)
    weight = jax.ShapeDtypeStruct((1, depth, width), BF16)
    act = jax.ShapeDtypeStruct((1, chunk, depth), BF16)
    dma = pltpu.SemaphoreType.DMA
    return pl.pallas_call(
        functools.partial(kernel, dims),
        out_shape=(act, act, weight, weight, weight),
        in_specs=[hbm_spec] * 11 + [smem_spec],
        out_specs=(hbm_spec,) * 5,
        scratch_shapes=[
            pltpu.VMEM((3, ring) + slim, BF16),
            pltpu.VMEM(slim, BF16),
            pltpu.VMEM(wide, BF16),
            pltpu.VMEM(wide, BF16),
            pltpu.VMEM((3, depth, width), BF16),
            pltpu.VMEM((3, blocks[0], 1, blocks[1]), jnp.int32),
            pltpu.VMEM((3, 8, width), F32),
            pltpu.VMEM((3, ring) + wide, BF16),
            pltpu.VMEM((3, half) + wide, BF16),
            pltpu.VMEM((3, max(half - 1, 1)) + wide, BF16),
            pltpu.VMEM((4, ring) + wide, BF16),
            pltpu.VMEM((2, depth, ring * chunk), BF16),
            pltpu.VMEM((2, ring) + slim, BF16),
            pltpu.VMEM((2, ring - 1) + slim, BF16),
            pltpu.VMEM(slim, BF16),
            pltpu.VMEM(slim, BF16),
            pltpu.VMEM((3, depth, width), BF16),
            dma((11,)),
            dma((7, 2, half)),
            dma((7, 2, half)),
            dma((3, ring - 1)),
            dma((3, ring - 1)),
            dma((2, ring)),
            dma((2, ring - 1)),
            dma,
            dma,
            dma((4,)),
        ],
        compiler_params=pltpu.CompilerParams(
            collective_id=0, has_side_effects=True, vmem_limit_bytes=63 * 1024 * 1024
        ),
    )(*args[:8], *(jnp.transpose(mask, (1, 0, 2)) for mask in args[8:11]), args[11])


def solution(mesh):
    tokens = P("pipe", "col", "row")
    grid = P("pipe", "row", "col")
    in_specs = (tokens, tokens, grid, grid, tokens) + (grid,) * 6 + (P(),)
    out_specs = (tokens, tokens, grid, grid, grid)
    return jax.shard_map(on_device, mesh=mesh, in_specs=in_specs, out_specs=out_specs, check_vma=False)
```

```python
import functools

import jax
import jax.numpy as jnp
from jax import lax
from jax.experimental import pallas as pl
from jax.experimental.pallas import tpu as pltpu
from jax.sharding import PartitionSpec as P

BLOCK = 128
BF16 = jnp.bfloat16
F32 = jnp.float32
MESH = pl.DeviceIdType.MESH
VMEM_LIMIT = 63 * 1024 * 1024
GU, DH, HF, DD, HB = range(5)
IN_X, IN_COT, IN_SAVED = range(3)
OUT_Y, OUT_DX = range(2)


def kernel(
    dims,
    fwd_in, saved_in, saved_gate, saved_up, grad_out,
    w_gate, w_up, w_down,
    mask_gate, mask_up, mask_down, counts,
    handoff, outward, grad_gate, grad_up, grad_down,
    acts, go_v, sg_v, su_v, weights, mask_v, mask_rows,
    part_gu, part_dh, full_hf, full_dd, full_hb,
    land_gu_a, land_gu_b, land_dh_a, land_dh_b, turned,
    outs, out_land, message, leaving, stage,
    load_sem, z_send, z_recv, g_send, g_recv, f_send, f_recv,
    p_send, p_recv, store_sem,
):
    ring, nx, chunk, depth, width = dims
    half = ring // 2
    row = lax.axis_index("row")
    col = lax.axis_index("col")
    pipe = lax.axis_index("pipe")
    y, x = col // nx, lax.rem(col, nx)
    right, left = lax.rem(row + 1, ring), lax.rem(row + ring - 1, ring)

    def along_x(d):
        return {"col": y * nx + lax.rem(x + d, nx)}

    def along_y(d):
        return {"col": lax.rem(y + d, nx) * nx + x}

    barrier = pltpu.get_barrier_semaphore()
    peers = [{"row": right}, {"row": left}, {"pipe": 1 - pipe}]
    peers += [along_x(d) for d in range(1, nx)] + [along_y(d) for d in range(1, nx)]
    for peer in peers:
        pl.semaphore_signal(barrier, inc=1, device_id=peer, device_id_type=MESH)

    masks = (mask_gate, mask_up, mask_down)
    moves = [
        (saved_gate.at[0], sg_v),
        (saved_up.at[0], su_v),
        (grad_out.at[0], go_v),
        (fwd_in.at[0], acts.at[IN_X, y, x]),
        (saved_in.at[0], acts.at[IN_SAVED, y, x]),
    ]
    moves += [(mask, mask_v.at[k]) for k, mask in enumerate(masks)]
    moves += [(w.at[0], weights.at[k]) for k, w in enumerate((w_gate, w_up, w_down))]
    loads = [pltpu.make_async_copy(src, dst, load_sem.at[k]) for k, (src, dst) in enumerate(moves)]
    for load in loads:
        load.start()

    pl.semaphore_wait(barrier, len(peers))

    def remote(src, dst, send_sem, recv_sem, device):
        return pltpu.make_async_remote_copy(
            src_ref=src, dst_ref=dst, send_sem=send_sem, recv_sem=recv_sem,
            device_id=device, device_id_type=MESH,
        )

    sums = {GU: (part_gu, land_gu_a, land_gu_b), DH: (part_dh, land_dh_a, land_dh_b)}
    fulls = {HF: full_hf, DD: full_dd, HB: full_hb}

    def arms(stream):
        longer = 1 if stream in (GU, DD) else -1
        return ((longer, half), (-longer, half - 1))

    def z_copy(stream, arm, step):
        d, n = arms(stream)[arm]
        if stream in sums:
            src = sums[stream][0].at[(d * (n - step)) % ring]
            dst = sums[stream][1 + arm].at[step]
        else:
            src = fulls[stream].at[(-d * step) % ring]
            dst = fulls[stream].at[(-d * (step + 1)) % ring]
        return remote(
            src, dst, z_send.at[stream], z_recv.at[stream, arm, step],
            {"row": right if d == 1 else left},
        )

    def z_step(stream, step):
        for arm in range(2):
            d, n = arms(stream)[arm]
            if 0 < step <= n:
                z_copy(stream, arm, step - 1).wait_recv()
                if stream in sums and step < n:
                    part = sums[stream][0]
                    slot = (d * (n - step)) % ring
                    land = sums[stream][1 + arm][step - 1]
                    part[slot] = (part[slot].astype(F32) + land.astype(F32)).astype(BF16)
            if step < n:
                z_copy(stream, arm, step).start()

    def z_finish(stream):
        ref = (sums[stream][0] if stream in sums else fulls[stream]).at[pl.ds(0, ring - 1)]
        remote(ref, ref, z_send.at[stream], z_recv.at[stream, 0, 0], {"row": right}).wait_send()

    def reduced(stream):
        part, land_a, land_b = sums[stream]
        return (
            part[0].astype(F32) + land_a[half - 1].astype(F32) + land_b[half - 2].astype(F32)
        )

    cut = chunk // 2
    halves = (pl.ds(0, cut), pl.ds(cut, cut))

    def gather_start(which, phase, source=None):
        buf = acts.at[which]
        for d in range(1, nx):
            for h, rows in enumerate(halves):
                if phase == 0:
                    dst = buf.at[y, x, rows]
                    src = dst if source is None else source.at[rows]
                    device = along_x(d) if h == 0 else along_y(d)
                else:
                    src = dst = buf.at[y, :, rows] if h == 0 else buf.at[:, x, rows]
                    device = along_y(d) if h == 0 else along_x(d)
                remote(src, dst, g_send.at[which], g_recv.at[which, phase], device).start()

    def gather_wait(which, phase):
        buf = acts.at[which]
        ref = buf.at[0, pl.ds(0, nx - 1)] if phase == 0 else buf.at[pl.ds(0, nx - 1)]
        remote(ref, ref, g_send.at[which], g_recv.at[which, phase], along_x(1)).wait_recv()

    def fold_start(which, j):
        owner = lax.rem(row + j, ring)
        index = lax.max(lax.rem(col - owner + ring, ring) - 1, 0)

        @pl.when(owner != col)
        def _():
            remote(
                outs.at[which, j], out_land.at[which, index],
                f_send.at[which], f_recv.at[which], {"col": owner},
            ).start()

    def fold_all(which):
        return remote(
            outs.at[which, pl.ds(0, ring - 1)], out_land.at[which],
            f_send.at[which], f_recv.at[which], along_x(1),
        )

    def fold_end(which):
        fold_all(which).wait_recv()
        total = outs[which, lax.rem(col - row + ring, ring)].astype(F32)
        for d in range(1, ring):
            total += out_land[which, d - 1].astype(F32)
        return total

    def expand_mask(k):
        for i in range(depth // BLOCK):
            row_mask = [
                jnp.broadcast_to(mask_v[k, i, :, b:b + 1].astype(F32), (1, BLOCK))
                for b in range(width // BLOCK)
            ]
            mask_rows[k, i:i + 1, :] = jnp.concatenate(row_mask, axis=1)

    def mask_row(k, i):
        return mask_rows[k, i:i + 1, :]

    def apply_mask(k):
        loads[5 + k].wait()
        expand_mask(k)
        loads[8 + k].wait()
        for i in range(depth // BLOCK):
            at = pl.ds(i * BLOCK, BLOCK)
            weights[k, at] = (weights[k, at].astype(F32) * mask_row(k, i)).astype(BF16)

    def rows_of(which, slots):
        chunks = [lax.rem(row + j, ring) for j in slots]
        return jnp.concatenate([acts[which, t // nx, lax.rem(t, nx)] for t in chunks], axis=0)

    quarter = ring // 4
    first_slots = [(half - quarter // 2 + k) % ring for k in range(quarter)]
    groups = [[(j + g * quarter) % ring for j in first_slots] for g in (0, 3, 1, 2)]

    def partials(which, slots, part, ks):
        lhs = rows_of(which, slots)
        for u, k in enumerate(ks):
            product = jnp.dot(lhs, weights[k], preferred_element_type=F32).astype(BF16)
            for m, j in enumerate(slots):
                part[j, u] = product[m * chunk:(m + 1) * chunk]

    def back_product(which, slots):
        total = None
        for full, u, k in (((full_hf, 0, 2),), ((full_dd, 0, 0), (full_dd, 1, 1)))[which]:
            lhs = jnp.concatenate([full[j, u] for j in slots], axis=0)
            term = lax.dot_general(
                lhs, weights[k], (((1,), (1,)), ((), ())), preferred_element_type=F32
            )
            total = term if total is None else total + term
        total = total.astype(BF16)
        for m, j in enumerate(slots):
            outs[which, j] = total[m * chunk:(m + 1) * chunk]
            fold_start(which, j)

    def turn(k, which):
        for g in range(0, ring, quarter):
            slots = range(g, g + quarter)
            turned[k, :, pl.ds(g * chunk, quarter * chunk)] = rows_of(which, slots).T

    stores = []

    def weight_grad(k, full, u, index, out):
        rhs = full[:, u].reshape(ring * chunk, width)
        for i in range(depth // BLOCK):
            at = pl.ds(i * BLOCK, BLOCK)
            product = jnp.dot(turned[k, at], rhs, preferred_element_type=F32)
            stage[index, at] = (product * mask_row(index, i)).astype(BF16)
        store = pltpu.make_async_copy(stage.at[index], out.at[0], store_sem.at[index])
        store.start()
        stores.append(store)

    gather_start(IN_X, 0, fwd_in.at[0])
    loads[0].wait()
    loads[1].wait()
    gate_b, up_b = sg_v[...].astype(F32), su_v[...].astype(F32)
    full_hb[0, 0] = (gate_b * jax.nn.sigmoid(gate_b) * up_b).astype(BF16)
    z_step(HB, 0)
    loads[2].wait()
    positions = col * chunk + lax.broadcasted_iota(jnp.int32, (chunk, depth), 0)
    acts[IN_COT, y, x] = jnp.where(positions < counts[1], go_v[...].astype(F32), 0.0).astype(BF16)
    gather_start(IN_COT, 0)
    loads[3].wait()
    apply_mask(0)
    gather_wait(IN_X, 0)
    gather_start(IN_X, 1)
    z_step(HB, 1)
    gather_wait(IN_COT, 0)
    gather_start(IN_COT, 1)
    apply_mask(1)
    apply_mask(2)
    z_step(HB, 2)
    gather_wait(IN_X, 1)
    partials(IN_X, groups[0], part_gu, (0, 1))
    z_step(GU, 0)
    for slots in groups[1:]:
        partials(IN_X, slots, part_gu, (0, 1))
    z_step(HB, 3)
    gather_wait(IN_COT, 1)
    partials(IN_COT, groups[0], part_dh, (2,))
    z_step(DH, 0)
    for slots in groups[1:]:
        partials(IN_COT, slots, part_dh, (2,))
    loads[4].wait()
    gather_start(IN_SAVED, 0)
    for s in range(1, half + 1):
        z_step(GU, s)
        if s > 1:
            z_step(DH, s - 1)
        if s == 1:
            turn(0, IN_COT)
        if s == 2:
            gather_wait(IN_SAVED, 0)
            gather_start(IN_SAVED, 1)
            z_step(HB, 4)
    gather_wait(IN_SAVED, 1)
    gate_up = reduced(GU)
    gate_f, up_f = gate_up[0], gate_up[1]
    full_hf[0, 0] = (gate_f * jax.nn.sigmoid(gate_f) * up_f).astype(BF16)
    z_step(HF, 0)
    z_step(DH, half)
    dhid = reduced(DH)[0]
    gate_b, up_b = sg_v[...].astype(F32), su_v[...].astype(F32)
    sig = jax.nn.sigmoid(gate_b)
    full_dd[0, 0] = (dhid * up_b * sig * (1.0 + gate_b * (1.0 - sig))).astype(BF16)
    full_dd[0, 1] = (dhid * gate_b * sig).astype(BF16)
    z_step(DD, 0)
    z_step(HB, 5)
    turn(1, IN_SAVED)
    pending = [0]
    for s in range(1, half + 1):
        z_step(HF, s)
        z_step(DD, s)
        pending += [s, ring - s] if s < half else [s]
        if s % 2 == 0 or s >= half - 1:
            back_product(OUT_Y, pending)
            back_product(OUT_DX, pending)
            pending = []
        if s == min(4, half):
            z_step(HB, 6)
    weight_grad(1, full_dd, 0, 0, grad_gate)
    z_step(HB, 7)
    weight_grad(1, full_dd, 1, 1, grad_up)
    ffn = fold_end(OUT_Y)
    back = fold_end(OUT_DX)
    result_y = jnp.where(positions < counts[0], acts[IN_X, y, x].astype(F32) + ffn, 0.0).astype(BF16)
    result_dx = (acts[IN_COT, y, x].astype(F32) + back).astype(BF16)
    first = jnp.full((chunk, depth), pipe, jnp.int32) == 0
    message[...] = jnp.where(first, result_y.astype(F32), result_dx.astype(F32)).astype(BF16)
    leaving[...] = jnp.where(first, result_dx.astype(F32), result_y.astype(F32)).astype(BF16)
    swap = remote(message, handoff.at[0], p_send, p_recv, {"pipe": 1 - pipe})
    swap.start()
    stores.append(pltpu.make_async_copy(leaving, outward.at[0], store_sem.at[3]))
    stores[-1].start()
    z_step(HB, 8)
    weight_grad(0, full_hb, 0, 2, grad_down)
    for stream in (GU, DH, HF, DD, HB):
        z_finish(stream)
    for which in (IN_X, IN_COT, IN_SAVED):
        ref = outs.at[0, pl.ds(0, ring - 1)]
        remote(ref, ref, g_send.at[which], g_recv.at[which, 0], along_x(1)).wait_send()
    for which in (OUT_Y, OUT_DX):
        fold_all(which).wait_send()
    swap.wait()
    for store in stores:
        store.wait()


def copy_out(*refs):
    sources, targets, staged = refs[:5], refs[5:10], refs[10:15]
    load_sem, store_sem = refs[15:]
    loads, stores = [], []
    for k in (2, 3, 4, 0, 1):
        rows = sources[k].shape[1]
        pieces = 3 if rows % 48 == 0 and rows > 64 else 1
        for p in range(pieces):
            at = pl.ds(p * (rows // pieces), rows // pieces)
            n = len(loads)
            loads.append(pltpu.make_async_copy(sources[k].at[0, at], staged[k].at[at], load_sem.at[n]))
            stores.append(pltpu.make_async_copy(staged[k].at[at], targets[k].at[0, at], store_sem.at[n]))
    for load in loads:
        load.start()
    for load, store in zip(loads, stores):
        load.wait()
        store.start()
    for store in stores:
        store.wait()


def on_device(*args):
    fwd_in, saved_gate = args[0], args[2]
    _, chunk, depth = fwd_in.shape
    _, chunk_r, width = saved_gate.shape
    ring = lax.axis_size("row")
    nx = 1
    while nx * nx < ring:
        nx += 1
    assert chunk == chunk_r and ring == lax.axis_size("col") == nx * nx
    half = ring // 2
    dims = (ring, nx, chunk, depth, width)
    wide = (chunk, width)
    slim = (chunk, depth)
    blocks = (depth // BLOCK, width // BLOCK)
    hbm_spec = pl.BlockSpec(memory_space=pltpu.HBM)
    smem_spec = pl.BlockSpec(memory_space=pltpu.SMEM)
    weight = jax.ShapeDtypeStruct((1, depth, width), BF16)
    act = jax.ShapeDtypeStruct((1, chunk, depth), BF16)
    shapes = (act, act, weight, weight, weight)
    dma = pltpu.SemaphoreType.DMA
    results = pl.pallas_call(
        functools.partial(kernel, dims),
        out_shape=shapes,
        in_specs=[hbm_spec] * 11 + [smem_spec],
        out_specs=(hbm_spec,) * 5,
        scratch_shapes=[
            pltpu.VMEM((3, nx, nx) + slim, BF16),
            pltpu.VMEM(slim, BF16),
            pltpu.VMEM(wide, BF16),
            pltpu.VMEM(wide, BF16),
            pltpu.VMEM((3, depth, width), BF16),
            pltpu.VMEM((3, blocks[0], 1, blocks[1]), jnp.int32),
            pltpu.VMEM((3, 8, width), F32),
            pltpu.VMEM((ring, 2) + wide, BF16),
            pltpu.VMEM((ring, 1) + wide, BF16),
            pltpu.VMEM((ring, 1) + wide, BF16),
            pltpu.VMEM((ring, 2) + wide, BF16),
            pltpu.VMEM((ring, 1) + wide, BF16),
            pltpu.VMEM((half, 2) + wide, BF16),
            pltpu.VMEM((half - 1, 2) + wide, BF16),
            pltpu.VMEM((half, 1) + wide, BF16),
            pltpu.VMEM((half - 1, 1) + wide, BF16),
            pltpu.VMEM((2, depth, ring * chunk), BF16),
            pltpu.VMEM((2, ring) + slim, BF16),
            pltpu.VMEM((2, ring - 1) + slim, BF16),
            pltpu.VMEM(slim, BF16),
            pltpu.VMEM(slim, BF16),
            pltpu.VMEM((3, depth, width), BF16),
            dma((11,)),
            dma((5,)),
            dma((5, 2, half)),
            dma((3,)),
            dma((3, 2)),
            dma((2,)),
            dma((2,)),
            dma,
            dma,
            dma((4,)),
        ],
        compiler_params=pltpu.CompilerParams(
            collective_id=0, has_side_effects=True, vmem_limit_bytes=VMEM_LIMIT
        ),
    )(*args[:8], *(jnp.transpose(mask, (1, 0, 2)) for mask in args[8:11]), args[11])
    return pl.pallas_call(
        copy_out,
        out_shape=shapes,
        in_specs=[hbm_spec] * 5,
        out_specs=(hbm_spec,) * 5,
        scratch_shapes=[pltpu.VMEM(shape.shape[1:], BF16) for shape in shapes] + [dma((11,)), dma((11,))],
        compiler_params=pltpu.CompilerParams(vmem_limit_bytes=VMEM_LIMIT),
    )(*results)


def solution(mesh):
    tokens = P("pipe", "col", "row")
    grid = P("pipe", "row", "col")
    in_specs = (tokens, tokens, grid, grid, tokens) + (grid,) * 6 + (P(),)
    out_specs = (tokens, tokens, grid, grid, grid)
    return jax.shard_map(on_device, mesh=mesh, in_specs=in_specs, out_specs=out_specs, check_vma=False)
```

```python
import functools

import jax
import jax.numpy as jnp
from jax import lax
from jax.experimental import pallas as pl
from jax.experimental.pallas import tpu as pltpu
from jax.sharding import PartitionSpec as P

BLOCK = 128
BF16 = jnp.bfloat16
F32 = jnp.float32
MESH = pl.DeviceIdType.MESH
VMEM_LIMIT = 63 * 1024 * 1024
GATE, UP, DH, HF, DG, DU, HB = range(7)
PIECES = (2, 2, 2, 2, 2, 2, 2)
IN_X, IN_COT, IN_SAVED = range(3)
OUT_Y, OUT_DX = range(2)


def kernel(
    dims,
    fwd_in, saved_in, saved_gate, saved_up, grad_out,
    w_gate, w_up, w_down,
    mask_gate, mask_up, mask_down, counts,
    handoff, outward, grad_gate, grad_up, grad_down,
    acts, go_v, sg_v, su_v, weights, mask_v, mask_rows,
    part, land_a, land_b, full, turned,
    outs, out_land, message, leaving, stage,
    load_sem, z_send, z_recv, g_send, g_recv, f_send, f_recv,
    p_send, p_recv, store_sem,
):
    ring, nx, chunk, depth, width = dims
    half = ring // 2
    row = lax.axis_index("row")
    col = lax.axis_index("col")
    pipe = lax.axis_index("pipe")
    y, x = col // nx, lax.rem(col, nx)
    right, left = lax.rem(row + 1, ring), lax.rem(row + ring - 1, ring)

    def along_x(d):
        return {"col": y * nx + lax.rem(x + d, nx)}

    def along_y(d):
        return {"col": lax.rem(y + d, nx) * nx + x}

    barrier = pltpu.get_barrier_semaphore()
    peers = [{"row": right}, {"row": left}, {"pipe": 1 - pipe}]
    peers += [along_x(d) for d in range(1, nx)] + [along_y(d) for d in range(1, nx)]
    for peer in peers:
        pl.semaphore_signal(barrier, inc=1, device_id=peer, device_id_type=MESH)

    masks = (mask_gate, mask_up, mask_down)
    moves = [
        (saved_gate.at[0], sg_v),
        (saved_up.at[0], su_v),
        (grad_out.at[0], go_v),
        (fwd_in.at[0], acts.at[IN_X, y, x]),
        (saved_in.at[0], acts.at[IN_SAVED, y, x]),
    ]
    moves += [(mask, mask_v.at[k]) for k, mask in enumerate(masks)]
    moves += [(w.at[0], weights.at[k]) for k, w in enumerate((w_gate, w_up, w_down))]
    loads = [pltpu.make_async_copy(src, dst, load_sem.at[k]) for k, (src, dst) in enumerate(moves)]
    for load in loads:
        load.start()

    pl.semaphore_wait(barrier, len(peers))

    def remote(src, dst, send_sem, recv_sem, device):
        return pltpu.make_async_remote_copy(
            src_ref=src, dst_ref=dst, send_sem=send_sem, recv_sem=recv_sem,
            device_id=device, device_id_type=MESH,
        )

    def arms(stream):
        longer = 1 if stream % 2 == 0 else -1
        return ((longer, half), (-longer, half - 1))

    def rows_at(stream, h):
        size = chunk // PIECES[stream]
        return pl.ds(h * size, size)

    def z_copy(stream, arm, step, h):
        d, n = arms(stream)[arm]
        rows = rows_at(stream, h)
        if stream <= DH:
            src = part.at[stream, (d * (n - step)) % ring, rows]
            dst = (land_a, land_b)[arm].at[stream, step, rows]
        else:
            src = full.at[stream - HF, (-d * step) % ring, rows]
            dst = full.at[stream - HF, (-d * (step + 1)) % ring, rows]
        index = (ring - 1) * sum(PIECES[:stream]) + (arm * half + step) * PIECES[stream] + h
        return remote(
            src, dst, z_send.at[stream], z_recv.at[index], {"row": right if d == 1 else left}
        )

    def z_step(stream, step):
        for h in range(PIECES[stream]):
            rows = rows_at(stream, h)
            for arm in range(2):
                d, n = arms(stream)[arm]
                if 0 < step <= n:
                    z_copy(stream, arm, step - 1, h).wait_recv()
                    if stream <= DH and step < n:
                        slot = (d * (n - step)) % ring
                        land = (land_a, land_b)[arm][stream, step - 1, rows].astype(F32)
                        part[stream, slot, rows] = (part[stream, slot, rows].astype(F32) + land).astype(BF16)
                if step < n:
                    z_copy(stream, arm, step, h).start()

    def z_finish(stream):
        ref = full.at[0, pl.ds(0, ring - 1)]
        remote(ref, ref, z_send.at[stream], z_recv.at[0], {"row": right}).wait_send()

    def reduced(stream):
        return (
            part[stream, 0].astype(F32)
            + land_a[stream, half - 1].astype(F32)
            + land_b[stream, half - 2].astype(F32)
        )

    cut = chunk // 2
    halves = (pl.ds(0, cut), pl.ds(cut, cut))

    def gather_start(which, phase, source=None):
        buf = acts.at[which]
        for d in range(1, nx):
            for h, rows in enumerate(halves):
                if phase == 0:
                    dst = buf.at[y, x, rows]
                    src = dst if source is None else source.at[rows]
                    device = along_x(d) if h == 0 else along_y(d)
                else:
                    src = dst = buf.at[y, :, rows] if h == 0 else buf.at[:, x, rows]
                    device = along_y(d) if h == 0 else along_x(d)
                remote(src, dst, g_send.at[which], g_recv.at[which, phase], device).start()

    def gather_wait(which, phase):
        buf = acts.at[which]
        ref = buf.at[0, pl.ds(0, nx - 1)] if phase == 0 else buf.at[pl.ds(0, nx - 1)]
        remote(ref, ref, g_send.at[which], g_recv.at[which, phase], along_x(1)).wait_recv()

    def fold_start(which, j):
        owner = lax.rem(row + j, ring)
        index = lax.max(lax.rem(col - owner + ring, ring) - 1, 0)

        @pl.when(owner != col)
        def _():
            remote(
                outs.at[which, j], out_land.at[which, index],
                f_send.at[which], f_recv.at[which], {"col": owner},
            ).start()

    def fold_all(which):
        return remote(
            outs.at[which, pl.ds(0, ring - 1)], out_land.at[which],
            f_send.at[which], f_recv.at[which], along_x(1),
        )

    def fold_end(which):
        fold_all(which).wait_recv()
        total = outs[which, lax.rem(col - row + ring, ring)].astype(F32)
        for d in range(1, ring):
            total += out_land[which, d - 1].astype(F32)
        return total

    def expand_mask(k):
        for i in range(depth // BLOCK):
            row_mask = [
                jnp.broadcast_to(mask_v[k, i, :, b:b + 1].astype(F32), (1, BLOCK))
                for b in range(width // BLOCK)
            ]
            mask_rows[k, i:i + 1, :] = jnp.concatenate(row_mask, axis=1)

    def mask_row(k, i):
        return mask_rows[k, i:i + 1, :]

    def apply_mask(k):
        loads[5 + k].wait()
        expand_mask(k)
        loads[8 + k].wait()
        for i in range(depth // BLOCK):
            at = pl.ds(i * BLOCK, BLOCK)
            weights[k, at] = (weights[k, at].astype(F32) * mask_row(k, i)).astype(BF16)

    def rows_of(which, slots):
        chunks = [lax.rem(row + j, ring) for j in slots]
        return jnp.concatenate([acts[which, t // nx, lax.rem(t, nx)] for t in chunks], axis=0)

    quarter = ring // 4
    first_slots = [(half - quarter // 2 + k) % ring for k in range(quarter)]
    groups = [[(j + g * quarter) % ring for j in first_slots] for g in (0, 3, 1, 2)]

    def partials(which, slots, streams):
        lhs = rows_of(which, slots)
        for stream in streams:
            product = jnp.dot(lhs, weights[stream], preferred_element_type=F32).astype(BF16)
            for m, j in enumerate(slots):
                part[stream, j] = product[m * chunk:(m + 1) * chunk]

    def back_product(which, slots):
        total = None
        for stream, k in (((HF, 2),), ((DG, 0), (DU, 1)))[which]:
            lhs = jnp.concatenate([full[stream - HF, j] for j in slots], axis=0)
            term = lax.dot_general(
                lhs, weights[k], (((1,), (1,)), ((), ())), preferred_element_type=F32
            )
            total = term if total is None else total + term
        total = total.astype(BF16)
        for m, j in enumerate(slots):
            outs[which, j] = total[m * chunk:(m + 1) * chunk]
            fold_start(which, j)

    def turn(k, which):
        for g in range(0, ring, quarter):
            slots = range(g, g + quarter)
            turned[k, :, pl.ds(g * chunk, quarter * chunk)] = rows_of(which, slots).T

    stores = []

    def weight_grad(k, stream, index, out):
        rhs = full[stream - HF].reshape(ring * chunk, width)
        for i in range(depth // BLOCK):
            at = pl.ds(i * BLOCK, BLOCK)
            product = jnp.dot(turned[k, at], rhs, preferred_element_type=F32)
            stage[index, at] = (product * mask_row(index, i)).astype(BF16)
        store = pltpu.make_async_copy(stage.at[index], out.at[0], store_sem.at[index])
        store.start()
        stores.append(store)

    gather_start(IN_X, 0, fwd_in.at[0])
    loads[0].wait()
    loads[1].wait()
    gate_b, up_b = sg_v[...].astype(F32), su_v[...].astype(F32)
    full[HB - HF, 0] = (gate_b * jax.nn.sigmoid(gate_b) * up_b).astype(BF16)
    z_step(HB, 0)
    loads[2].wait()
    positions = col * chunk + lax.broadcasted_iota(jnp.int32, (chunk, depth), 0)
    acts[IN_COT, y, x] = jnp.where(positions < counts[1], go_v[...].astype(F32), 0.0).astype(BF16)
    gather_start(IN_COT, 0)
    loads[3].wait()
    apply_mask(0)
    gather_wait(IN_X, 0)
    gather_start(IN_X, 1)
    z_step(HB, 1)
    gather_wait(IN_COT, 0)
    gather_start(IN_COT, 1)
    apply_mask(1)
    apply_mask(2)
    z_step(HB, 2)
    gather_wait(IN_X, 1)
    partials(IN_X, groups[0], (GATE, UP))
    z_step(GATE, 0)
    z_step(UP, 0)
    for slots in groups[1:]:
        partials(IN_X, slots, (GATE, UP))
    z_step(HB, 3)
    gather_wait(IN_COT, 1)
    partials(IN_COT, groups[0], (DH,))
    z_step(DH, 0)
    for slots in groups[1:]:
        partials(IN_COT, slots, (DH,))
    loads[4].wait()
    gather_start(IN_SAVED, 0)
    for s in range(1, half + 1):
        z_step(GATE, s)
        z_step(UP, s)
        if s > 1:
            z_step(DH, s - 1)
        if s == 1:
            turn(0, IN_COT)
        if s == 2:
            gather_wait(IN_SAVED, 0)
            gather_start(IN_SAVED, 1)
            z_step(HB, 4)
    gather_wait(IN_SAVED, 1)
    gate_f, up_f = reduced(GATE), reduced(UP)
    full[0, 0] = (gate_f * jax.nn.sigmoid(gate_f) * up_f).astype(BF16)
    z_step(HF, 0)
    z_step(DH, half)
    dhid = reduced(DH)
    gate_b, up_b = sg_v[...].astype(F32), su_v[...].astype(F32)
    sig = jax.nn.sigmoid(gate_b)
    full[DG - HF, 0] = (dhid * up_b * sig * (1.0 + gate_b * (1.0 - sig))).astype(BF16)
    full[DU - HF, 0] = (dhid * gate_b * sig).astype(BF16)
    z_step(DG, 0)
    z_step(DU, 0)
    z_step(HB, 5)
    turn(1, IN_SAVED)
    pending = [0]
    for s in range(1, half + 1):
        z_step(HF, s)
        z_step(DG, s)
        z_step(DU, s)
        pending += [s, ring - s] if s < half else [s]
        if s % 2 == 0 or s >= half - 1:
            back_product(OUT_Y, pending)
            back_product(OUT_DX, pending)
            pending = []
        if s == min(4, half):
            z_step(HB, 6)
    weight_grad(1, DG, 0, grad_gate)
    z_step(HB, 7)
    weight_grad(1, DU, 1, grad_up)
    ffn = fold_end(OUT_Y)
    back = fold_end(OUT_DX)
    result_y = jnp.where(positions < counts[0], acts[IN_X, y, x].astype(F32) + ffn, 0.0).astype(BF16)
    result_dx = (acts[IN_COT, y, x].astype(F32) + back).astype(BF16)
    first = jnp.full((chunk, depth), pipe, jnp.int32) == 0
    message[...] = jnp.where(first, result_y.astype(F32), result_dx.astype(F32)).astype(BF16)
    leaving[...] = jnp.where(first, result_dx.astype(F32), result_y.astype(F32)).astype(BF16)
    swap = remote(message, handoff.at[0], p_send, p_recv, {"pipe": 1 - pipe})
    swap.start()
    stores.append(pltpu.make_async_copy(leaving, outward.at[0], store_sem.at[3]))
    stores[-1].start()
    z_step(HB, 8)
    weight_grad(0, HB, 2, grad_down)
    for stream in range(7):
        z_finish(stream)
    for which in (IN_X, IN_COT, IN_SAVED):
        ref = outs.at[0, pl.ds(0, ring - 1)]
        remote(ref, ref, g_send.at[which], g_recv.at[which, 0], along_x(1)).wait_send()
    for which in (OUT_Y, OUT_DX):
        fold_all(which).wait_send()
    swap.wait()
    for store in stores:
        store.wait()


def copy_out(*refs):
    sources, targets, staged = refs[:5], refs[5:10], refs[10:15]
    load_sem, store_sem = refs[15:]
    loads, stores = [], []
    for k in (2, 3, 4, 0, 1):
        rows = sources[k].shape[1]
        pieces = 3 if rows % 48 == 0 and rows > 64 else 1
        for p in range(pieces):
            at = pl.ds(p * (rows // pieces), rows // pieces)
            n = len(loads)
            loads.append(pltpu.make_async_copy(sources[k].at[0, at], staged[k].at[at], load_sem.at[n]))
            stores.append(pltpu.make_async_copy(staged[k].at[at], targets[k].at[0, at], store_sem.at[n]))
    for load in loads:
        load.start()
    for load, store in zip(loads, stores):
        load.wait()
        store.start()
    for store in stores:
        store.wait()


def on_device(*args):
    fwd_in, saved_gate = args[0], args[2]
    _, chunk, depth = fwd_in.shape
    _, chunk_r, width = saved_gate.shape
    ring = lax.axis_size("row")
    nx = 1
    while nx * nx < ring:
        nx += 1
    assert chunk == chunk_r and ring == lax.axis_size("col") == nx * nx
    half = ring // 2
    dims = (ring, nx, chunk, depth, width)
    wide = (chunk, width)
    slim = (chunk, depth)
    blocks = (depth // BLOCK, width // BLOCK)
    hbm_spec = pl.BlockSpec(memory_space=pltpu.HBM)
    smem_spec = pl.BlockSpec(memory_space=pltpu.SMEM)
    weight = jax.ShapeDtypeStruct((1, depth, width), BF16)
    act = jax.ShapeDtypeStruct((1, chunk, depth), BF16)
    shapes = (act, act, weight, weight, weight)
    dma = pltpu.SemaphoreType.DMA
    results = pl.pallas_call(
        functools.partial(kernel, dims),
        out_shape=shapes,
        in_specs=[hbm_spec] * 11 + [smem_spec],
        out_specs=(hbm_spec,) * 5,
        scratch_shapes=[
            pltpu.VMEM((3, nx, nx) + slim, BF16),
            pltpu.VMEM(slim, BF16),
            pltpu.VMEM(wide, BF16),
            pltpu.VMEM(wide, BF16),
            pltpu.VMEM((3, depth, width), BF16),
            pltpu.VMEM((3, blocks[0], 1, blocks[1]), jnp.int32),
            pltpu.VMEM((3, 8, width), F32),
            pltpu.VMEM((3, ring) + wide, BF16),
            pltpu.VMEM((3, half) + wide, BF16),
            pltpu.VMEM((3, half - 1) + wide, BF16),
            pltpu.VMEM((4, ring) + wide, BF16),
            pltpu.VMEM((2, depth, ring * chunk), BF16),
            pltpu.VMEM((2, ring) + slim, BF16),
            pltpu.VMEM((2, ring - 1) + slim, BF16),
            pltpu.VMEM(slim, BF16),
            pltpu.VMEM(slim, BF16),
            pltpu.VMEM((3, depth, width), BF16),
            dma((11,)),
            dma((7,)),
            dma(((ring - 1) * sum(PIECES),)),
            dma((3,)),
            dma((3, 2)),
            dma((2,)),
            dma((2,)),
            dma,
            dma,
            dma((4,)),
        ],
        compiler_params=pltpu.CompilerParams(
            collective_id=0, has_side_effects=True, vmem_limit_bytes=VMEM_LIMIT
        ),
    )(*args[:8], *(jnp.transpose(mask, (1, 0, 2)) for mask in args[8:11]), args[11])
    return pl.pallas_call(
        copy_out,
        out_shape=shapes,
        in_specs=[hbm_spec] * 5,
        out_specs=(hbm_spec,) * 5,
        scratch_shapes=[pltpu.VMEM(shape.shape[1:], BF16) for shape in shapes] + [dma((11,)), dma((11,))],
        compiler_params=pltpu.CompilerParams(vmem_limit_bytes=VMEM_LIMIT),
    )(*results)


def solution(mesh):
    tokens = P("pipe", "col", "row")
    grid = P("pipe", "row", "col")
    in_specs = (tokens, tokens, grid, grid, tokens) + (grid,) * 6 + (P(),)
    out_specs = (tokens, tokens, grid, grid, grid)
    return jax.shard_map(on_device, mesh=mesh, in_specs=in_specs, out_specs=out_specs, check_vma=False)
```

```python
import functools

import jax
import jax.numpy as jnp
from jax import lax
from jax.experimental import pallas as pl
from jax.experimental.pallas import tpu as pltpu
from jax.sharding import PartitionSpec as P

BLOCK = 128
BF16 = jnp.bfloat16
F32 = jnp.float32
MESH = pl.DeviceIdType.MESH
VMEM_LIMIT = 61 * 1024 * 1024 + 900 * 1024
GATE, UP, DH, HF, DG, DU, HB = range(7)
PIECES = (2, 2, 2, 2, 2, 2, 2)
IN_X, IN_COT, IN_SAVED = range(3)
OUT_Y, OUT_DX = range(2)


def kernel(
    dims,
    fwd_in, saved_in, saved_gate, saved_up, grad_out,
    w_gate, w_up, w_down,
    mask_gate, mask_up, mask_down, counts,
    handoff, outward, grad_gate, grad_up, grad_down,
    acts, go_v, sg_v, su_v, weights, mask_v, mask_rows,
    part, land_a, land_b, full, turned,
    outs, out_land, message,
    load_sem, z_send, z_recv, g_send, g_recv, f_send, f_recv,
    p_send, p_recv,
):
    ring, nx, chunk, depth, width = dims
    half = ring // 2
    row = lax.axis_index("row")
    col = lax.axis_index("col")
    pipe = lax.axis_index("pipe")
    y, x = col // nx, lax.rem(col, nx)
    right, left = lax.rem(row + 1, ring), lax.rem(row + ring - 1, ring)

    def along_x(d):
        return {"col": y * nx + lax.rem(x + d, nx)}

    def along_y(d):
        return {"col": lax.rem(y + d, nx) * nx + x}

    barrier = pltpu.get_barrier_semaphore()
    peers = [{"row": right}, {"row": left}, {"pipe": 1 - pipe}]
    peers += [along_x(d) for d in range(1, nx)] + [along_y(d) for d in range(1, nx)]
    for peer in peers:
        pl.semaphore_signal(barrier, inc=1, device_id=peer, device_id_type=MESH)

    masks = (mask_gate, mask_up, mask_down)
    moves = [
        (saved_gate.at[0], sg_v),
        (saved_up.at[0], su_v),
        (grad_out.at[0], go_v),
        (fwd_in.at[0], acts.at[IN_X, y, x]),
        (saved_in.at[0], acts.at[IN_SAVED, y, x]),
    ]
    moves += [(mask, mask_v.at[k]) for k, mask in enumerate(masks)]
    moves += [(w.at[0], weights.at[k]) for k, w in enumerate((w_gate, w_up, w_down))]
    loads = [pltpu.make_async_copy(src, dst, load_sem.at[k]) for k, (src, dst) in enumerate(moves)]
    for load in loads:
        load.start()

    pl.semaphore_wait(barrier, len(peers))

    def remote(src, dst, send_sem, recv_sem, device):
        return pltpu.make_async_remote_copy(
            src_ref=src, dst_ref=dst, send_sem=send_sem, recv_sem=recv_sem,
            device_id=device, device_id_type=MESH,
        )

    def arms(stream):
        longer = 1 if stream % 2 == 0 else -1
        return ((longer, half), (-longer, half - 1))

    def rows_at(stream, h):
        size = chunk // PIECES[stream]
        return pl.ds(h * size, size)

    def z_copy(stream, arm, step, h):
        d, n = arms(stream)[arm]
        rows = rows_at(stream, h)
        if stream <= DH:
            src = part.at[stream, (d * (n - step)) % ring, rows]
            dst = (land_a, land_b)[arm].at[stream, step, rows]
        else:
            src = full.at[stream - HF, (-d * step) % ring, rows]
            dst = full.at[stream - HF, (-d * (step + 1)) % ring, rows]
        shared = stream if stream <= DH else stream - HF
        index = (ring - 1) * sum(PIECES[:shared]) + (arm * half + step) * PIECES[stream] + h
        return remote(
            src, dst, z_send.at[stream], z_recv.at[index], {"row": right if d == 1 else left}
        )

    def z_piece(stream, step, h, arm):
        rows = rows_at(stream, h)
        d, n = arms(stream)[arm]
        if 0 < step <= n:
            z_copy(stream, arm, step - 1, h).wait_recv()
            if stream <= DH and step < n:
                slot = (d * (n - step)) % ring
                land = (land_a, land_b)[arm][stream, step - 1, rows].astype(F32)
                part[stream, slot, rows] = (part[stream, slot, rows].astype(F32) + land).astype(BF16)
        if step < n:
            z_copy(stream, arm, step, h).start()

    def z_steps(*steps):
        for h in range(2):
            for stream, step in steps:
                for arm in range(2):
                    z_piece(stream, step, h, arm)

    def z_step(stream, step):
        for h in range(PIECES[stream]):
            for arm in range(2):
                z_piece(stream, step, h, arm)

    def z_finish(stream):
        ref = full.at[0, pl.ds(0, ring - 1)]
        remote(ref, ref, z_send.at[stream], z_recv.at[0], {"row": right}).wait_send()

    def reduced(stream):
        return (
            part[stream, 0].astype(F32)
            + land_a[stream, half - 1].astype(F32)
            + land_b[stream, half - 2].astype(F32)
        )

    cut = chunk // 2
    halves = (pl.ds(0, cut), pl.ds(cut, cut))

    def gather_start(which, phase, source=None):
        buf = acts.at[which]
        for d in range(1, nx):
            for h, rows in enumerate(halves):
                if phase == 0:
                    dst = buf.at[y, x, rows]
                    src = dst if source is None else source.at[rows]
                    device = along_x(d) if h == 0 else along_y(d)
                else:
                    src = dst = buf.at[y, :, rows] if h == 0 else buf.at[:, x, rows]
                    device = along_y(d) if h == 0 else along_x(d)
                remote(src, dst, g_send.at[which], g_recv.at[which, phase], device).start()

    def gather_wait(which, phase):
        buf = acts.at[which]
        ref = buf.at[0, pl.ds(0, nx - 1)] if phase == 0 else buf.at[pl.ds(0, nx - 1)]
        remote(ref, ref, g_send.at[which], g_recv.at[which, phase], along_x(1)).wait_recv()

    def fold_start(which, j):
        owner = lax.rem(row + j, ring)
        index = lax.max(lax.rem(col - owner + ring, ring) - 1, 0)

        @pl.when(owner != col)
        def _():
            remote(
                outs.at[which, j], out_land.at[which, index],
                f_send.at[which], f_recv.at[which], {"col": owner},
            ).start()

    def fold_all(which):
        return remote(
            outs.at[which, pl.ds(0, ring - 1)], out_land.at[which],
            f_send.at[which], f_recv.at[which], along_x(1),
        )

    def fold_end(which):
        fold_all(which).wait_recv()
        total = outs[which, lax.rem(col - row + ring, ring)].astype(F32)
        for d in range(1, ring):
            total += out_land[which, d - 1].astype(F32)
        return total

    def expand_mask(k):
        for i in range(depth // BLOCK):
            row_mask = [
                jnp.broadcast_to(mask_v[k, i, :, b:b + 1].astype(F32), (1, BLOCK))
                for b in range(width // BLOCK)
            ]
            mask_rows[k, i:i + 1, :] = jnp.concatenate(row_mask, axis=1)

    def mask_row(k, i):
        return mask_rows[k, i:i + 1, :]

    def apply_mask(k):
        loads[5 + k].wait()
        expand_mask(k)
        loads[8 + k].wait()
        for i in range(depth // BLOCK):
            at = pl.ds(i * BLOCK, BLOCK)
            weights[k, at] = (weights[k, at].astype(F32) * mask_row(k, i)).astype(BF16)

    def rows_of(which, slots):
        chunks = [lax.rem(row + j, ring) for j in slots]
        return jnp.concatenate([acts[which, t // nx, lax.rem(t, nx)] for t in chunks], axis=0)

    quarter = ring // 4
    first_slots = [(half - quarter // 2 + k) % ring for k in range(quarter)]
    groups = [[(j + g * quarter) % ring for j in first_slots] for g in (0, 3, 1, 2)]

    def partials(which, slots, streams):
        lhs = rows_of(which, slots)
        for stream in streams:
            product = jnp.dot(lhs, weights[stream], preferred_element_type=F32).astype(BF16)
            for m, j in enumerate(slots):
                part[stream, j] = product[m * chunk:(m + 1) * chunk]

    def back_product(which, slots):
        total = None
        for stream, k in (((HF, 2),), ((DG, 0), (DU, 1)))[which]:
            lhs = jnp.concatenate([full[stream - HF, j] for j in slots], axis=0)
            term = lax.dot_general(
                lhs, weights[k], (((1,), (1,)), ((), ())), preferred_element_type=F32
            )
            total = term if total is None else total + term
        total = total.astype(BF16)
        for m, j in enumerate(slots):
            outs[which, j] = total[m * chunk:(m + 1) * chunk]
            fold_start(which, j)

    def turn(k, which):
        for g in range(0, ring, quarter):
            slots = range(g, g + quarter)
            turned[k, :, pl.ds(g * chunk, quarter * chunk)] = rows_of(which, slots).T


    def weight_grad(k, stream, index, out):
        rhs = full[stream - HF].reshape(ring * chunk, width)
        for i in range(depth // BLOCK):
            at = pl.ds(i * BLOCK, BLOCK)
            product = jnp.dot(turned[k, at], rhs, preferred_element_type=F32)
            out[0, at] = (product * mask_row(index, i)).astype(BF16)

    gather_start(IN_X, 0, fwd_in.at[0])
    loads[0].wait()
    loads[1].wait()
    gate_b, up_b = sg_v[...].astype(F32), su_v[...].astype(F32)
    full[HB - HF, 0] = (gate_b * jax.nn.sigmoid(gate_b) * up_b).astype(BF16)
    z_step(HB, 0)
    loads[2].wait()
    positions = col * chunk + lax.broadcasted_iota(jnp.int32, (chunk, depth), 0)
    acts[IN_COT, y, x] = jnp.where(positions < counts[1], go_v[...].astype(F32), 0.0).astype(BF16)
    gather_start(IN_COT, 0)
    loads[3].wait()
    apply_mask(0)
    gather_wait(IN_X, 0)
    gather_start(IN_X, 1)
    z_step(HB, 1)
    gather_wait(IN_COT, 0)
    gather_start(IN_COT, 1)
    apply_mask(1)
    apply_mask(2)
    z_step(HB, 2)
    gather_wait(IN_X, 1)
    partials(IN_X, groups[0], (GATE, UP))
    z_step(GATE, 0)
    z_step(UP, 0)
    for slots in groups[1:]:
        partials(IN_X, slots, (GATE, UP))
    z_step(HB, 3)
    z_step(GATE, 1)
    z_step(UP, 1)
    gather_wait(IN_COT, 1)
    partials(IN_COT, groups[0], (DH,))
    z_step(DH, 0)
    for slots in groups[1:]:
        partials(IN_COT, slots, (DH,))
    loads[4].wait()
    gather_start(IN_SAVED, 0)
    for s in range(1, half + 1):
        if s > 1:
            z_steps((GATE, s), (UP, s), (DH, s - 1))
        if s == 1:
            z_step(HB, 4)
            turn(0, IN_COT)
        if s == half:
            z_step(HB, 5)
        if s == 2:
            gather_wait(IN_SAVED, 0)
            gather_start(IN_SAVED, 1)
    gather_wait(IN_SAVED, 1)
    gate_f, up_f = reduced(GATE), reduced(UP)
    full[0, 0] = (gate_f * jax.nn.sigmoid(gate_f) * up_f).astype(BF16)
    z_step(HF, 0)
    z_step(DH, half)
    dhid = reduced(DH)
    gate_b, up_b = sg_v[...].astype(F32), su_v[...].astype(F32)
    sig = jax.nn.sigmoid(gate_b)
    full[DG - HF, 0] = (dhid * up_b * sig * (1.0 + gate_b * (1.0 - sig))).astype(BF16)
    full[DU - HF, 0] = (dhid * gate_b * sig).astype(BF16)
    z_step(DG, 0)
    z_step(DU, 0)
    z_step(HB, 6)
    turn(1, IN_SAVED)
    pending = [0]
    for s in range(1, half + 1):
        z_steps((HF, s), (DG, s), (DU, s))
        pending += [s, ring - s] if s < half else [s]
        if s % 2 == 0 or s >= half - 1:
            back_product(OUT_Y, pending)
            back_product(OUT_DX, pending)
            pending = []
        if s == half - 1:
            z_step(HB, 7)
    weight_grad(1, DG, 0, grad_gate)
    weight_grad(1, DU, 1, grad_up)
    ffn = fold_end(OUT_Y)
    back = fold_end(OUT_DX)
    result_y = jnp.where(positions < counts[0], acts[IN_X, y, x].astype(F32) + ffn, 0.0).astype(BF16)
    result_dx = (acts[IN_COT, y, x].astype(F32) + back).astype(BF16)
    first = jnp.full((chunk, depth), pipe, jnp.int32) == 0
    message[...] = jnp.where(first, result_y.astype(F32), result_dx.astype(F32)).astype(BF16)
    outward[0] = jnp.where(first, result_dx.astype(F32), result_y.astype(F32)).astype(BF16)
    swap = remote(message, handoff.at[0], p_send, p_recv, {"pipe": 1 - pipe})
    swap.start()
    z_step(HB, 8)
    weight_grad(0, HB, 2, grad_down)
    for stream in range(7):
        z_finish(stream)
    for which in (IN_X, IN_COT, IN_SAVED):
        ref = outs.at[0, pl.ds(0, ring - 1)]
        remote(ref, ref, g_send.at[which], g_recv.at[which, 0], along_x(1)).wait_send()
    for which in (OUT_Y, OUT_DX):
        fold_all(which).wait_send()
    swap.wait()


def copy_out(*refs):
    copies = [pltpu.make_async_copy(refs[k], refs[5 + k], refs[10].at[k]) for k in range(5)]
    for copy in copies:
        copy.start()
    for copy in copies:
        copy.wait()


def on_device(*args):
    fwd_in, saved_gate = args[0], args[2]
    _, chunk, depth = fwd_in.shape
    _, chunk_r, width = saved_gate.shape
    ring = lax.axis_size("row")
    nx = 1
    while nx * nx < ring:
        nx += 1
    assert chunk == chunk_r and ring == lax.axis_size("col") == nx * nx
    half = ring // 2
    dims = (ring, nx, chunk, depth, width)
    wide = (chunk, width)
    slim = (chunk, depth)
    blocks = (depth // BLOCK, width // BLOCK)
    hbm_spec = pl.BlockSpec(memory_space=pltpu.HBM)
    vmem_spec = pl.BlockSpec(memory_space=pltpu.VMEM)
    smem_spec = pl.BlockSpec(memory_space=pltpu.SMEM)
    weight_shape, act_shape = (1, depth, width), (1, chunk, depth)
    dma = pltpu.SemaphoreType.DMA
    results = pl.pallas_call(
        functools.partial(kernel, dims),
        out_shape=(pltpu.VMEM(act_shape, BF16),) * 2 + (pltpu.VMEM(weight_shape, BF16),) * 3,
        in_specs=[hbm_spec] * 11 + [smem_spec],
        out_specs=(vmem_spec,) * 5,
        scratch_shapes=[
            pltpu.VMEM((3, nx, nx) + slim, BF16),
            pltpu.VMEM(slim, BF16),
            pltpu.VMEM(wide, BF16),
            pltpu.VMEM(wide, BF16),
            pltpu.VMEM((3, depth, width), BF16),
            pltpu.VMEM((3, blocks[0], 1, blocks[1]), jnp.int32),
            pltpu.VMEM((3, 8, width), F32),
            pltpu.VMEM((3, ring) + wide, BF16),
            pltpu.VMEM((3, half) + wide, BF16),
            pltpu.VMEM((3, half - 1) + wide, BF16),
            pltpu.VMEM((4, ring) + wide, BF16),
            pltpu.VMEM((2, depth, ring * chunk), BF16),
            pltpu.VMEM((2, ring) + slim, BF16),
            pltpu.VMEM((2, ring - 1) + slim, BF16),
            pltpu.VMEM(slim, BF16),
            dma((11,)),
            dma((7,)),
            dma(((ring - 1) * sum(PIECES[HF:]),)),
            dma((3,)),
            dma((3, 2)),
            dma((2,)),
            dma((2,)),
            dma,
            dma,
        ],
        compiler_params=pltpu.CompilerParams(
            collective_id=0, has_side_effects=True, vmem_limit_bytes=VMEM_LIMIT
        ),
    )(*args[:8], *(jnp.transpose(mask, (1, 0, 2)) for mask in args[8:11]), args[11])

    return pl.pallas_call(
        copy_out,
        out_shape=tuple(jax.ShapeDtypeStruct(result.shape, BF16) for result in results),
        in_specs=[pl.BlockSpec(memory_space=pl.ANY)] * 5,
        out_specs=(hbm_spec,) * 5,
        scratch_shapes=[dma((5,))],
        compiler_params=pltpu.CompilerParams(vmem_limit_bytes=8 * 1024 * 1024),
    )(*results)


def solution(mesh):
    tokens = P("pipe", "col", "row")
    grid = P("pipe", "row", "col")
    in_specs = (tokens, tokens, grid, grid, tokens) + (grid,) * 6 + (P(),)
    out_specs = (tokens, tokens, grid, grid, grid)
    return jax.shard_map(on_device, mesh=mesh, in_specs=in_specs, out_specs=out_specs, check_vma=False)
```

```python
import functools

import jax
import jax.numpy as jnp
from jax import lax
from jax.experimental import pallas as pl
from jax.experimental.pallas import tpu as pltpu
from jax.sharding import PartitionSpec as P

BLOCK = 128
LEAD = 2
BF16 = jnp.bfloat16
F32 = jnp.float32
MESH = pl.DeviceIdType.MESH
VMEM_LIMIT = 61 * 1024 * 1024 + 900 * 1024
GATE, UP, DH, HF, DG, DU, HB = range(7)
PIECES = (2, 2, 2, 2, 2, 2, 2)
IN_X, IN_COT, IN_SAVED = range(3)
OUT_Y, OUT_DX = range(2)


def kernel(
    dims,
    fwd_in, saved_in, saved_gate, saved_up, grad_out,
    w_gate, w_up, w_down,
    mask_gate, mask_up, mask_down, counts,
    handoff, outward, grad_gate, grad_up, grad_down,
    acts, go_v, sg_v, su_v, weights, mask_v, mask_rows,
    part, land_a, land_b, full, turned,
    outs, out_land, message,
    load_sem, z_send, z_recv, g_send, g_recv, f_send, f_recv,
    p_send, p_recv, pace,
):
    ring, nx, chunk, depth, width = dims
    half = ring // 2
    row = lax.axis_index("row")
    col = lax.axis_index("col")
    pipe = lax.axis_index("pipe")
    y, x = col // nx, lax.rem(col, nx)
    right, left = lax.rem(row + 1, ring), lax.rem(row + ring - 1, ring)

    def along_x(d):
        return {"col": y * nx + lax.rem(x + d, nx)}

    def along_y(d):
        return {"col": lax.rem(y + d, nx) * nx + x}

    barrier = pltpu.get_barrier_semaphore()
    peers = [{"row": right}, {"row": left}, {"pipe": 1 - pipe}]
    peers += [along_x(d) for d in range(1, nx)] + [along_y(d) for d in range(1, nx)]
    for peer in peers:
        pl.semaphore_signal(barrier, inc=1, device_id=peer, device_id_type=MESH)

    masks = (mask_gate, mask_up, mask_down)
    moves = [
        (saved_gate.at[0], sg_v),
        (saved_up.at[0], su_v),
        (grad_out.at[0], go_v),
        (fwd_in.at[0], acts.at[IN_X, y, x]),
        (saved_in.at[0], acts.at[IN_SAVED, y, x]),
    ]
    moves += [(mask, mask_v.at[k]) for k, mask in enumerate(masks)]
    moves += [(w.at[0], weights.at[k]) for k, w in enumerate((w_gate, w_up, w_down))]
    loads = [pltpu.make_async_copy(src, dst, load_sem.at[k]) for k, (src, dst) in enumerate(moves)]
    for load in loads:
        load.start()

    pl.semaphore_wait(barrier, len(peers))

    def remote(src, dst, send_sem, recv_sem, device):
        return pltpu.make_async_remote_copy(
            src_ref=src, dst_ref=dst, send_sem=send_sem, recv_sem=recv_sem,
            device_id=device, device_id_type=MESH,
        )

    def arms(stream):
        longer = 1 if stream % 2 == 0 else -1
        return ((longer, half), (-longer, half - 1))

    def rows_at(stream, h):
        size = chunk // PIECES[stream]
        return pl.ds(h * size, size)

    def z_copy(stream, arm, step, h):
        d, n = arms(stream)[arm]
        rows = rows_at(stream, h)
        if stream <= DH:
            src = part.at[stream, (d * (n - step)) % ring, rows]
            dst = (land_a, land_b)[arm].at[stream, step, rows]
        else:
            src = full.at[stream - HF, (-d * step) % ring, rows]
            dst = full.at[stream - HF, (-d * (step + 1)) % ring, rows]
        shared = stream if stream <= DH else stream - HF
        index = (shared * 2 + arm) * 4 * 2 + (step % 4) * 2 + h
        return remote(
            src, dst, z_send.at[stream], z_recv.at[index], {"row": right if d == 1 else left}
        )

    def z_piece(stream, step, h, arm):
        rows = rows_at(stream, h)
        d, n = arms(stream)[arm]
        if 0 < step <= n:
            z_copy(stream, arm, step - 1, h).wait_recv()
            if stream <= DH and step < n:
                slot = (d * (n - step)) % ring
                land = (land_a, land_b)[arm][stream, step - 1, rows].astype(F32)
                part[stream, slot, rows] = (part[stream, slot, rows].astype(F32) + land).astype(BF16)
        if step < n:
            z_copy(stream, arm, step, h).start()

    def z_steps(*steps):
        for h in range(2):
            for stream, step in steps:
                for arm in range(2):
                    z_piece(stream, step, h, arm)

    def z_step(stream, step):
        for h in range(PIECES[stream]):
            for arm in range(2):
                z_piece(stream, step, h, arm)

    def z_part(*pieces):
        for stream, step, h in pieces:
            for arm in range(2):
                z_piece(stream, step, h, arm)

    def z_finish(stream):
        ref = full.at[0, pl.ds(0, ring - 1)]
        remote(ref, ref, z_send.at[stream], z_recv.at[0], {"row": right}).wait_send()

    def reduced(stream):
        return (
            part[stream, 0].astype(F32)
            + land_a[stream, half - 1].astype(F32)
            + land_b[stream, half - 2].astype(F32)
        )

    cut = chunk // 2
    halves = (pl.ds(0, cut), pl.ds(cut, cut))

    def gather_start(which, phase, source=None):
        buf = acts.at[which]
        for d in range(1, nx):
            for h, rows in enumerate(halves):
                if phase == 0:
                    dst = buf.at[y, x, rows]
                    src = dst if source is None else source.at[rows]
                    device = along_x(d) if h == 0 else along_y(d)
                else:
                    src = dst = buf.at[y, :, rows] if h == 0 else buf.at[:, x, rows]
                    device = along_y(d) if h == 0 else along_x(d)
                remote(src, dst, g_send.at[which], g_recv.at[which, phase], device).start()

    def gather_wait(which, phase):
        buf = acts.at[which]
        ref = buf.at[0, pl.ds(0, nx - 1)] if phase == 0 else buf.at[pl.ds(0, nx - 1)]
        remote(ref, ref, g_send.at[which], g_recv.at[which, phase], along_x(1)).wait_recv()

    def fold_start(which, j):
        owner = lax.rem(row + j, ring)
        index = lax.max(lax.rem(col - owner + ring, ring) - 1, 0)

        @pl.when(owner != col)
        def _():
            remote(
                outs.at[which, j], out_land.at[which, index],
                f_send.at[which], f_recv.at[which], {"col": owner},
            ).start()

    def fold_all(which):
        return remote(
            outs.at[which, pl.ds(0, ring - 1)], out_land.at[which],
            f_send.at[which], f_recv.at[which], along_x(1),
        )

    def fold_end(which):
        fold_all(which).wait_recv()
        total = outs[which, lax.rem(col - row + ring, ring)].astype(F32)
        for d in range(1, ring):
            total += out_land[which, d - 1].astype(F32)
        return total

    def expand_mask(k):
        for i in range(depth // BLOCK):
            row_mask = [
                jnp.broadcast_to(mask_v[k, i, :, b:b + 1].astype(F32), (1, BLOCK))
                for b in range(width // BLOCK)
            ]
            mask_rows[k, i:i + 1, :] = jnp.concatenate(row_mask, axis=1)

    def mask_row(k, i):
        return mask_rows[k, i:i + 1, :]

    def apply_mask(k):
        loads[5 + k].wait()
        expand_mask(k)
        loads[8 + k].wait()
        for i in range(depth // BLOCK):
            at = pl.ds(i * BLOCK, BLOCK)
            weights[k, at] = (weights[k, at].astype(F32) * mask_row(k, i)).astype(BF16)

    def rows_of(which, slots):
        chunks = [lax.rem(row + j, ring) for j in slots]
        return jnp.concatenate([acts[which, t // nx, lax.rem(t, nx)] for t in chunks], axis=0)

    quarter = ring // 4
    first_slots = [(half - quarter // 2 + k) % ring for k in range(quarter)]
    groups = [[(j + g * quarter) % ring for j in first_slots] for g in (0, 3, 1, 2)]

    def partials(which, slots, streams):
        lhs = rows_of(which, slots)
        for stream in streams:
            product = jnp.dot(lhs, weights[stream], preferred_element_type=F32).astype(BF16)
            for m, j in enumerate(slots):
                part[stream, j] = product[m * chunk:(m + 1) * chunk]

    def back_product(which, slots):
        total = None
        for stream, k in (((HF, 2),), ((DG, 0), (DU, 1)))[which]:
            lhs = jnp.concatenate([full[stream - HF, j] for j in slots], axis=0)
            term = lax.dot_general(
                lhs, weights[k], (((1,), (1,)), ((), ())), preferred_element_type=F32
            )
            total = term if total is None else total + term
        total = total.astype(BF16)
        for m, j in enumerate(slots):
            outs[which, j] = total[m * chunk:(m + 1) * chunk]
            fold_start(which, j)

    def turn(k, which):
        for g in range(0, ring, quarter):
            slots = range(g, g + quarter)
            turned[k, :, pl.ds(g * chunk, quarter * chunk)] = rows_of(which, slots).T


    def weight_grad(k, stream, index, out):
        rhs = full[stream - HF].reshape(ring * chunk, width)
        for i in range(depth // BLOCK):
            at = pl.ds(i * BLOCK, BLOCK)
            product = jnp.dot(turned[k, at], rhs, preferred_element_type=F32)
            out[0, at] = (product * mask_row(index, i)).astype(BF16)

    def round_start(number):
        if number > LEAD:
            @pl.when(pipe == 1)
            def _():
                pl.semaphore_wait(pace, 1)

    def round_end(number):
        if number <= 2 * half - LEAD:
            @pl.when(pipe == 0)
            def _():
                pl.semaphore_signal(pace, inc=1, device_id={"pipe": 1 - pipe}, device_id_type=MESH)

    gather_start(IN_X, 0, fwd_in.at[0])
    loads[0].wait()
    loads[1].wait()
    gate_b, up_b = sg_v[...].astype(F32), su_v[...].astype(F32)
    full[HB - HF, 0] = (gate_b * jax.nn.sigmoid(gate_b) * up_b).astype(BF16)
    z_step(HB, 0)
    loads[2].wait()
    positions = col * chunk + lax.broadcasted_iota(jnp.int32, (chunk, depth), 0)
    acts[IN_COT, y, x] = jnp.where(positions < counts[1], go_v[...].astype(F32), 0.0).astype(BF16)
    gather_start(IN_COT, 0)
    loads[3].wait()
    apply_mask(0)
    gather_wait(IN_X, 0)
    gather_start(IN_X, 1)
    z_step(HB, 1)
    gather_wait(IN_COT, 0)
    gather_start(IN_COT, 1)
    apply_mask(1)
    apply_mask(2)
    z_step(HB, 2)
    gather_wait(IN_X, 1)
    partials(IN_X, groups[0], (GATE, UP))
    z_part((GATE, 0, 0), (GATE, 0, 1), (UP, 0, 0))
    for slots in groups[1:]:
        partials(IN_X, slots, (GATE, UP))
    z_part((UP, 0, 1))
    z_step(HB, 3)
    z_part((GATE, 1, 0), (GATE, 1, 1), (UP, 1, 0))
    gather_wait(IN_COT, 1)
    for slots in groups:
        partials(IN_COT, slots, (DH,))
    loads[4].wait()
    gather_start(IN_SAVED, 0)
    turn(0, IN_COT)
    z_part((UP, 1, 1), (DH, 0, 0), (DH, 0, 1))
    for s in range(1, half + 1):
        round_start(s)
        if s > 1:
            z_part((GATE, s, 0), (GATE, s, 1), (UP, s, 0))
            z_part((UP, s, 1), (DH, s - 1, 0), (DH, s - 1, 1))
        round_end(s)
        if s == 1:
            z_step(HB, 4)
        if s == half:
            z_step(HB, 5)
        if s == 2:
            gather_wait(IN_SAVED, 0)
            gather_start(IN_SAVED, 1)
    gather_wait(IN_SAVED, 1)
    gate_f, up_f = reduced(GATE), reduced(UP)
    full[0, 0] = (gate_f * jax.nn.sigmoid(gate_f) * up_f).astype(BF16)
    z_step(HF, 0)
    z_step(DH, half)
    dhid = reduced(DH)
    gate_b, up_b = sg_v[...].astype(F32), su_v[...].astype(F32)
    sig = jax.nn.sigmoid(gate_b)
    full[DG - HF, 0] = (dhid * up_b * sig * (1.0 + gate_b * (1.0 - sig))).astype(BF16)
    full[DU - HF, 0] = (dhid * gate_b * sig).astype(BF16)
    z_step(DG, 0)
    z_step(DU, 0)
    z_step(HB, 6)
    turn(1, IN_SAVED)
    pending = [0]
    for s in range(1, half + 1):
        round_start(half + s)
        z_step(HF, s)
        z_step(DG, s)
        z_step(DU, s)
        round_end(half + s)
        pending += [s, ring - s] if s < half else [s]
        if s % 2 == 0 or s >= half - 1:
            back_product(OUT_Y, pending)
            back_product(OUT_DX, pending)
            pending = []
        if s == half - 1:
            z_step(HB, 7)
    weight_grad(1, DG, 0, grad_gate)
    weight_grad(1, DU, 1, grad_up)
    ffn = fold_end(OUT_Y)
    back = fold_end(OUT_DX)
    result_y = jnp.where(positions < counts[0], acts[IN_X, y, x].astype(F32) + ffn, 0.0).astype(BF16)
    result_dx = (acts[IN_COT, y, x].astype(F32) + back).astype(BF16)
    first = jnp.full((chunk, depth), pipe, jnp.int32) == 0
    message[...] = jnp.where(first, result_y.astype(F32), result_dx.astype(F32)).astype(BF16)
    outward[0] = jnp.where(first, result_dx.astype(F32), result_y.astype(F32)).astype(BF16)
    swap = remote(message, handoff.at[0], p_send, p_recv, {"pipe": 1 - pipe})
    swap.start()
    z_step(HB, 8)
    weight_grad(0, HB, 2, grad_down)
    for stream in range(7):
        z_finish(stream)
    for which in (IN_X, IN_COT, IN_SAVED):
        ref = outs.at[0, pl.ds(0, ring - 1)]
        remote(ref, ref, g_send.at[which], g_recv.at[which, 0], along_x(1)).wait_send()
    for which in (OUT_Y, OUT_DX):
        fold_all(which).wait_send()
    swap.wait()


def copy_out(*refs):
    copies = [pltpu.make_async_copy(refs[k], refs[5 + k], refs[10].at[k]) for k in range(5)]
    for copy in copies:
        copy.start()
    for copy in copies:
        copy.wait()


def on_device(*args):
    fwd_in, saved_gate = args[0], args[2]
    _, chunk, depth = fwd_in.shape
    _, chunk_r, width = saved_gate.shape
    ring = lax.axis_size("row")
    nx = 1
    while nx * nx < ring:
        nx += 1
    assert chunk == chunk_r and ring == lax.axis_size("col") == nx * nx
    half = ring // 2
    dims = (ring, nx, chunk, depth, width)
    wide = (chunk, width)
    slim = (chunk, depth)
    blocks = (depth // BLOCK, width // BLOCK)
    hbm_spec = pl.BlockSpec(memory_space=pltpu.HBM)
    vmem_spec = pl.BlockSpec(memory_space=pltpu.VMEM)
    smem_spec = pl.BlockSpec(memory_space=pltpu.SMEM)
    weight_shape, act_shape = (1, depth, width), (1, chunk, depth)
    dma = pltpu.SemaphoreType.DMA
    results = pl.pallas_call(
        functools.partial(kernel, dims),
        out_shape=(pltpu.VMEM(act_shape, BF16),) * 2 + (pltpu.VMEM(weight_shape, BF16),) * 3,
        in_specs=[hbm_spec] * 11 + [smem_spec],
        out_specs=(vmem_spec,) * 5,
        scratch_shapes=[
            pltpu.VMEM((3, nx, nx) + slim, BF16),
            pltpu.VMEM(slim, BF16),
            pltpu.VMEM(wide, BF16),
            pltpu.VMEM(wide, BF16),
            pltpu.VMEM((3, depth, width), BF16),
            pltpu.VMEM((3, blocks[0], 1, blocks[1]), jnp.int32),
            pltpu.VMEM((3, 8, width), F32),
            pltpu.VMEM((3, ring) + wide, BF16),
            pltpu.VMEM((3, half) + wide, BF16),
            pltpu.VMEM((3, half - 1) + wide, BF16),
            pltpu.VMEM((4, ring) + wide, BF16),
            pltpu.VMEM((2, depth, ring * chunk), BF16),
            pltpu.VMEM((2, ring) + slim, BF16),
            pltpu.VMEM((2, ring - 1) + slim, BF16),
            pltpu.VMEM(slim, BF16),
            dma((11,)),
            dma((7,)),
            dma((4 * 2 * 4 * 2,)),
            dma((3,)),
            dma((3, 2)),
            dma((2,)),
            dma((2,)),
            dma,
            dma,
            pltpu.SemaphoreType.REGULAR,
        ],
        compiler_params=pltpu.CompilerParams(
            collective_id=0, has_side_effects=True, vmem_limit_bytes=VMEM_LIMIT
        ),
    )(*args[:8], *(jnp.transpose(mask, (1, 0, 2)) for mask in args[8:11]), args[11])

    return pl.pallas_call(
        copy_out,
        out_shape=tuple(jax.ShapeDtypeStruct(result.shape, BF16) for result in results),
        in_specs=[pl.BlockSpec(memory_space=pl.ANY)] * 5,
        out_specs=(hbm_spec,) * 5,
        scratch_shapes=[dma((5,))],
        compiler_params=pltpu.CompilerParams(vmem_limit_bytes=8 * 1024 * 1024),
    )(*results)


def solution(mesh):
    tokens = P("pipe", "col", "row")
    grid = P("pipe", "row", "col")
    in_specs = (tokens, tokens, grid, grid, tokens) + (grid,) * 6 + (P(),)
    out_specs = (tokens, tokens, grid, grid, grid)
    return jax.shard_map(on_device, mesh=mesh, in_specs=in_specs, out_specs=out_specs, check_vma=False)
```
